1024 devices in a mesh: depth: 64 (over x, z), tile: 16 (over y, core).
Axes of the slice: x: 8, y: 8, z: 8, core: 2. Of those that a mesh axis runs over, the one named last changes fastest.
Arguments:
- features: bfloat16 [32, 256, 131072], P(None, 'depth', 'tile'), may hold values from -6 to 6
- ray_spans: int32 [2, 64, 131072], P(None, 'depth', 'tile'), may hold values from 0 to 4, as said below
- view_order: int32 [16], P('tile'), may hold values 0 or 1
- w_first: bfloat16 [128, 32], replicated, may hold values from -1 to 1
- b_first: float32 [128], replicated, may hold values from -3 to 3
- w_second: bfloat16 [128, 128], replicated, may hold values from -0.5 to 0.5
- b_second: float32 [128], replicated, may hold values from -3 to 3
- w_last: bfloat16 [4, 128], replicated, may hold values from -0.5 to 0.5
- b_last: float32 [4], replicated, may hold values from -3 to 3
Outputs:
- image: float32 [4, 131072], P(None, ('tile', 'depth'))
The draws below stay inside these ranges and needn't reach their ends.
Inputs may be any that keep to these rules, and one draw needn't show every extreme that they name: A ray samples positions ray_spans[0] to ray_spans[1] - 1 of its slab. Within each block of 1024 pixels (aligned, in one slab) either every ray has ray_spans[0] < ray_spans[1], or every ray has both equal to 0.
All inputs are finite; a program needn't handle non-finite values. No bound on the sum of `view_order` on one device may be relied on, other than what follows from the above.
Results may differ from the reference program's by a relative error of at most 0.00039.
Values may be sent and summed in bfloat16 or wider, within the bound.
A program may use at most 32 MiB of HBM per device.

```python
import jax
import jax.numpy as jnp
from jax import lax

CHANNELS = 32
HIDDEN_SIZE = 128
SLAB_SAMPLES = 4
PIX_DEV = 8192
BRICK_PIX = 1024
SLABS = 64
TILES = 16
PIXELS = 131072
SAMPLES = 256


def draw_ray_spans(key, part):
    key = jax.random.fold_in(key, 11)
    streams = jax.random.split(key, 4)
    brick_count = PIXELS // BRICK_PIX
    levels = jax.random.randint(streams[0], (SLABS, PIXELS // PIX_DEV), 1, 9)
    levels = jnp.repeat(levels, PIX_DEV // BRICK_PIX, axis=1)
    filled = jax.random.randint(streams[1], (SLABS, brick_count), 0, 8) < levels
    filled = jnp.repeat(filled, BRICK_PIX, axis=1)
    entries = jax.random.randint(streams[2], (SLABS, PIXELS), 0, SLAB_SAMPLES)
    lengths = 1 + jax.random.randint(streams[3], (SLABS, PIXELS), 0, SLAB_SAMPLES - entries)
    leaving = entries + lengths
    return jnp.stack([jnp.where(filled, entries, 0), jnp.where(filled, leaving, 0)]).astype(jnp.int32)


def set_ends(drawn, rng, least, largest):
    place = [jax.random.randint(jax.random.fold_in(rng, axis), (), 0, length) for axis, length in enumerate(drawn.shape)]
    main_axis = drawn.shape.index(max(drawn.shape))
    neighbour = place[:main_axis] + [(place[main_axis] + 1) % drawn.shape[main_axis]] + place[main_axis + 1:]
    return drawn.at[tuple(place)].set(least).at[tuple(neighbour)].set(largest)


def shard_levels(key, dims, shards, smallest, high):
    loudness = 1.0
    for axis_at, blocks in shards:
        draws = jax.random.uniform(jax.random.fold_in(jax.random.fold_in(key, 6), axis_at), (blocks,), jnp.float32, smallest / len(shards), high / len(shards))
        loudness = loudness * jnp.repeat(jnp.exp(draws), dims[axis_at] // blocks).reshape((-1,) + (1,) * (len(dims) - 1 - axis_at))
    return loudness


def scatter_about(rng, dims, scale, most, cuts=(), kind=jnp.bfloat16):
    loudness = shard_levels(rng, dims, cuts, -0.22, 0.18) if cuts else 1.0
    values = jax.random.normal(rng, dims, jnp.float32) * scale * loudness
    return jnp.minimum(jnp.maximum(values, -most), most).astype(kind)


def setup_inputs(seed: int = 0) -> dict:
    streams_of = jax.random.split(jax.random.key(seed), 10)
    features = scatter_about(streams_of[0], (CHANNELS, SAMPLES, PIXELS), 1.0, 6.0, ((1, 64), (2, 16)))
    ray_spans = draw_ray_spans(jax.random.fold_in(streams_of[9], 71), 0)
    view_order = set_ends((jax.random.randint(streams_of[2], (TILES,), 0, 2) < 1).astype(jnp.int32), jax.random.fold_in(streams_of[2], 1), 0, 1)
    w_first = scatter_about(streams_of[3], (HIDDEN_SIZE, CHANNELS), CHANNELS ** -0.5, 1.0)
    b_first = scatter_about(streams_of[4], (HIDDEN_SIZE,), 0.5, 3.0, (), jnp.float32)
    w_second = scatter_about(streams_of[5], (HIDDEN_SIZE, HIDDEN_SIZE), HIDDEN_SIZE ** -0.5, 0.5)
    b_second = scatter_about(streams_of[6], (HIDDEN_SIZE,), 0.5, 3.0, (), jnp.float32)
    w_last = scatter_about(streams_of[7], (4, HIDDEN_SIZE), HIDDEN_SIZE ** -0.5, 0.5)
    b_last = scatter_about(streams_of[8], (4,), 0.5, 3.0, (), jnp.float32)
    return {"features": features, "ray_spans": ray_spans, "view_order": view_order, "w_first": w_first, "b_first": b_first, "w_second": w_second, "b_second": b_second, "w_last": w_last, "b_last": b_last}


def stack_over(layers, flipped):
    layers = jnp.where(flipped == 1, layers[::-1], layers)
    remain = 1.0 - layers[:, 3]
    through = jnp.concatenate([jnp.ones_like(remain[:1]), jnp.cumprod(remain, axis=0)[:-1]], axis=0)
    return jnp.sum(through[:, None] * layers, axis=0)


def decode(weights, voxels, entries, leaving, flipped, spacing):
    w_first, b_first, w_second, b_second, w_last, b_last = weights
    channels, samples, columns = voxels.shape
    stacked = voxels.reshape(channels, samples * columns)
    first = jax.nn.relu(jnp.dot(w_first, stacked, preferred_element_type=jnp.float32) + b_first[:, None]).astype(jnp.bfloat16)
    second = jax.nn.relu(jnp.dot(w_second, first, preferred_element_type=jnp.float32) + b_second[:, None]).astype(jnp.bfloat16)
    output = (jnp.dot(w_last, second, preferred_element_type=jnp.float32) + b_last[:, None]).reshape(4, samples, columns)
    places = jnp.arange(samples, dtype=jnp.int32)[:, None]
    inside = (places >= entries[None, :]) & (places < leaving[None, :])
    opacity = jnp.where(inside, 1.0 - jnp.exp(-jax.nn.softplus(output[0]) * spacing), 0.0)
    shading = jax.nn.sigmoid(output[1:4])
    layers = jnp.concatenate([opacity[None] * shading, opacity[None]], axis=0)
    return stack_over(jnp.transpose(layers, (1, 0, 2)), flipped)


def reference(features, ray_spans, view_order, w_first, b_first, w_second, b_second, w_last, b_last):
    weights = (w_first, b_first, w_second, b_second, w_last, b_last)
    flipped = jnp.repeat(view_order, PIX_DEV)
    spacing = 6.0 / (SLAB_SAMPLES * SLABS)
    blocks = features.reshape(CHANNELS, SLABS, SLAB_SAMPLES, PIXELS)

    def render_slab(level):
        voxels = lax.dynamic_index_in_dim(blocks, level, 1, keepdims=False)
        bounds = lax.dynamic_index_in_dim(ray_spans, level, 1, keepdims=False)
        return decode(weights, voxels, bounds[0], bounds[1], flipped, spacing)

    layers = lax.map(render_slab, jnp.arange(SLABS, dtype=jnp.int32))
    return stack_over(layers, flipped)
```

```python
import functools

import jax
import jax.numpy as jnp
from jax import lax
from jax.experimental import pallas as pl
from jax.experimental.pallas import tpu as pltpu
from jax.sharding import PartitionSpec as P

BF = jnp.bfloat16
F = jnp.float32
BRICK = 1024
CH = 32
NCH = 256 // CH
UNITS = ((0, 0), (0, 1), (1, 0), (1, 1))
MESH = pl.DeviceIdType.MESH


def over(near, far):
    through = 1.0 - near[3]
    return [a + through * b for a, b in zip(near, far)]


def ordered(flip, first, second):
    near = [jnp.where(flip, b, a) for a, b in zip(first, second)]
    far = [jnp.where(flip, a, b) for a, b in zip(first, second)]
    return over(near, far)


def stack_samples(z_ref, spans, zrow, row, flip, b_last, spacing):
    entry = spans[0, pl.ds(row, 8), :]
    leave = spans[1, pl.ds(row, 8), :]
    remain, opacity = [], []
    for s in range(4):
        density = z_ref[pl.ds(zrow + 4 * s, 8, stride=16), :] + b_last[0]
        soft = jnp.maximum(density, 0.0) + jnp.log1p(jnp.exp(-jnp.abs(density)))
        kept = jnp.exp(soft * (-spacing))
        kept = jnp.where((entry <= s) & (leave > s), kept, 1.0)
        remain.append(kept)
        opacity.append(1.0 - kept)
    p01 = remain[0] * remain[1]
    p012 = p01 * remain[2]
    q32 = remain[3] * remain[2]
    q321 = q32 * remain[1]
    through = [
        jnp.where(flip, q321, 1.0),
        jnp.where(flip, q32, remain[0]),
        jnp.where(flip, remain[3], p01),
        jnp.where(flip, 1.0, p012),
    ]
    weight = [t * o for t, o in zip(through, opacity)]
    layers = []
    for ch in range(3):
        total = None
        for s in range(4):
            color = z_ref[pl.ds(zrow + 4 * s + 1 + ch, 8, stride=16), :] + b_last[1 + ch]
            term = weight[s] * (0.5 * jnp.tanh(0.5 * color) + 0.5)
            total = term if total is None else total + term
        layers.append(total)
    layers.append((weight[0] + weight[1]) + (weight[2] + weight[3]))
    return layers


def kernel(*refs, slabs):
    accs = []
    for m in range(2):
        accs += [pltpu.ACC(m)((CH, 256), F)] * (2 * NCH)
        accs += [pltpu.ACC(m)((16, 256), F)] * 2 + [pltpu.ACC(m)((128, 256), F)]
    pl.run_scoped(lambda *accs: body(*refs, accs=accs, slabs=slabs), *accs)


def body(
    x_hbm, spans, order, w1t, w2, w3, b1, b2, bl_ref, out,
    xbuf, xs, w1p, w2p, w3p, bias, z_ref, h1s, h2s, sent, taken, sem, send_sem, recv_sem,
    *, accs, slabs,
):
    n = 2 * NCH + 3
    acc1 = [accs[m * n : m * n + NCH] for m in range(2)]
    acc2 = [accs[m * n + NCH : m * n + 2 * NCH] for m in range(2)]
    acc3 = [accs[m * n + 2 * NCH : m * n + 2 * NCH + 2] for m in range(2)]
    accw = [accs[m * n + 2 * NCH + 2] for m in range(2)]
    bricks = 8
    me = lax.axis_index("depth")
    low = lax.rem(me, 8)
    high = lax.div(me, 8)
    spacing = 6.0 / (4 * slabs)

    def place(k):
        return lax.rem(high + 1 + k, 8)

    def xcopy(k):
        start = pl.multiple_of(place(k) * BRICK, BRICK)
        return pltpu.make_async_copy(x_hbm.at[:, :, pl.ds(start, BRICK)], xbuf.at[k], sem.at[k])

    for k in range(bricks):
        xcopy(k).start()

    barrier = pltpu.get_barrier_semaphore()

    def greet(j, _):
        peer = lax.rem(me + j, slabs)
        pl.semaphore_signal(barrier, inc=1, device_id={"depth": peer}, device_id_type=MESH)
        return 0

    lax.fori_loop(1, slabs, greet, 0)

    first = jnp.concatenate([w1t[...].astype(F), jnp.zeros((96, 128), F)], axis=0)
    first = jnp.transpose(first).astype(BF)
    first = jnp.concatenate([first, jnp.zeros((128, 128), BF)], axis=1)
    channel = lax.broadcasted_iota(jnp.int32, (256, 128), 0)
    column = lax.broadcasted_iota(jnp.int32, (256, 128), 1)
    zero = jnp.zeros((128, 128), BF)
    for q in range(2):
        spread = jnp.concatenate(
            [(column == channel * 4 + (2 * q + k)).astype(F).astype(BF) for k in range(2)], axis=1
        )
        pltpu.matmul_push_rhs(spread, 0, q)
        pltpu.matmul_acc_lhs(accw[q], first, load_staged_rhs=0)
    for q in range(2):
        wide = pltpu.matmul_pop(accw[q]).astype(BF)
        for k in range(2):
            for j in range(2):
                w1p[j, q, k * 128 : (k + 1) * 128, j * 128 : (j + 1) * 128] = wide[:, k * 128 : (k + 1) * 128]
                w1p[j, q, k * 128 : (k + 1) * 128, (1 - j) * 128 : (2 - j) * 128] = zero
    for k in range(2):
        w2p[k * 128 : (k + 1) * 128, k * 128 : (k + 1) * 128] = w2[...]
        w2p[k * 128 : (k + 1) * 128, (1 - k) * 128 : (2 - k) * 128] = zero
    last = w3[...].astype(F)
    none = jnp.zeros((4, 128), F)
    for q in range(2):
        left = jnp.concatenate([last if s == 2 * q else none for s in range(4)], axis=0)
        right = jnp.concatenate([last if s == 2 * q + 1 else none for s in range(4)], axis=0)
        w3p[q] = jnp.concatenate([left, right], axis=1).astype(BF)
    bias[0] = jnp.transpose(jnp.broadcast_to(b1[...], (128, 128)))
    bias[1] = jnp.transpose(jnp.broadcast_to(b2[...], (128, 128)))
    flip = jnp.full((8, 128), order[0], jnp.int32) == 1
    b_last = [bl_ref[i] for i in range(4)]

    def prep(k, m, j):
        if m == 0 and j == 0:
            xcopy(k).wait()
        tile = xbuf[k, :, :, m * 512 + j * 256 : m * 512 + (j + 1) * 256]
        xs[lax.rem(k, 2), m, j * 128 : (j + 1) * 128, :] = tile.reshape(128, 256)

    def settle(acc, layer, i, dst, m):
        r = (i * CH) % 128
        shift = bias[layer, r : r + CH, :]
        value = pltpu.matmul_pop(acc) + jnp.concatenate([shift, shift], axis=1)
        dst[m, i * CH : (i + 1) * CH, :] = jnp.maximum(value.astype(BF), jnp.zeros((), BF))

    def push_x(par, stage):
        for m in range(2):
            pltpu.matmul_push_rhs(xs[par, m], stage, m)

    def push_h(h, stage):
        for m in range(2):
            pltpu.matmul_push_rhs(h[m], stage, m)

    def layer_one(u, stage, drain):
        j, q = UNITS[u]
        for i in range(NCH):
            for m in range(2):
                pltpu.matmul_acc_lhs(
                    acc1[m][i], w1p[j, q, i * CH : (i + 1) * CH, :], load_staged_rhs=stage if i == 0 else None
                )
                if drain:
                    settle(acc2[m][i], 1, i, h2s, m)

    def layer_two(stage, drain):
        for i in range(NCH):
            for m in range(2):
                pltpu.matmul_acc_lhs(
                    acc2[m][i], w2p[i * CH : (i + 1) * CH, :], load_staged_rhs=stage if i == 0 else None
                )
                if drain:
                    settle(acc1[m][i], 0, i, h1s, m)

    def layer_three(u, stage, par):
        j, q = UNITS[u]
        for m in range(2):
            pltpu.matmul_acc_lhs(acc3[m][j], w3p[q], load_staged_rhs=stage)
        if q == 1:
            for m in range(2):
                value = pltpu.matmul_pop(acc3[m][j])
                t = 2 * m + j
                z_ref[pl.ds(par * 128 + 32 * t, 16), :] = value[:, :128]
                z_ref[pl.ds(par * 128 + 32 * t + 16, 16), :] = value[:, 128:]

    def drain_two():
        for i in range(NCH):
            for m in range(2):
                settle(acc2[m][i], 1, i, h2s, m)

    def brick(k, is_first=False, is_last=False, extra=None):
        par = lax.rem(k, 2)
        for u in range(4):
            begins = is_first and u == 0
            ends = is_last and u == 3
            base = (u * 3) % 2
            push_h(h1s, 1 - base)
            if not ends:
                layer_one((u + 1) % 4, base, not begins)
            else:
                drain_two()
            if not is_last:
                prep(k + 1, u % 2, u // 2)
            if u == 2 and extra:
                extra()
            if not begins:
                push_h(h2s, base)
            layer_two(1 - base, not ends)
            if u < 2:
                push_x(par, 1 - base)
            elif not is_last:
                push_x(1 - par, 1 - base)
            if not begins:
                if u > 0:
                    layer_three(u - 1, base, par)
                else:
                    layer_three(3, base, 1 - par)

    def send(k, j):
        chunk = lax.rem(low + j, 8)
        return pltpu.make_async_remote_copy(
            src_ref=sent.at[k * 8 + chunk],
            dst_ref=taken.at[me],
            send_sem=send_sem,
            recv_sem=recv_sem,
            device_id={"depth": place(k) * 8 + chunk},
            device_id_type=MESH,
        )

    def finish(k):
        row = pl.multiple_of(place(k) * 8, 8)
        layers = stack_samples(z_ref, spans, lax.rem(k, 2) * 128, row, flip, b_last, spacing)
        for ch in range(4):
            sent[pl.ds(k * 8, 8), ch, :] = layers[ch]

    def finish_send(k):
        finish(k)
        for j in range(8):
            send(k, j).start()

    for m in range(2):
        for j in range(2):
            prep(0, m, j)
    push_x(0, 1)
    for i in range(NCH):
        for m in range(2):
            pltpu.matmul_acc_lhs(
                acc1[m][i], w1p[0, 0, i * CH : (i + 1) * CH, :], load_staged_rhs=1 if i == 0 else None
            )
    push_x(0, 0)
    for i in range(NCH):
        for m in range(2):
            settle(acc1[m][i], 0, i, h1s, m)
    brick(0, is_first=True)
    pl.semaphore_wait(barrier, slabs - 1)

    def step(k, _):
        brick(k, extra=lambda: finish_send(k - 1))
        return 0

    lax.fori_loop(1, bricks - 1, step, 0)
    brick(bricks - 1, is_last=True, extra=lambda: finish_send(bricks - 2))
    drain_two()
    push_h(h2s, 0)
    layer_three(3, 0, (bricks - 1) % 2)
    finish(bricks - 1)
    for j in range(1, 8):
        send(bricks - 1, j).start()
    taken[me] = sent[(bricks - 1) * 8 + low]

    others = pltpu.make_async_remote_copy(
        src_ref=sent.at[pl.ds(0, slabs - 1)],
        dst_ref=taken.at[pl.ds(0, slabs - 1)],
        send_sem=send_sem,
        recv_sem=recv_sem,
        device_id={"depth": lax.rem(me + 1, slabs)},
        device_id_type=MESH,
    )
    others.wait_recv()
    groups = [[taken[pl.ds(k, 8, stride=8), ch, :] for ch in range(4)] for k in range(8)]
    while len(groups) > 1:
        groups = [ordered(flip, a, b) for a, b in zip(groups[::2], groups[1::2])]
    total = groups[0]
    for shift in (7, 6, 4):
        total = ordered(flip, total, [pltpu.roll(c, shift, 0) for c in total])
    out[...] = jnp.concatenate([c[0:1] for c in total], axis=0)
    others.wait_send()


def per_device(features, ray_spans, view_order, w_first, b_first, w_second, b_second, w_last, b_last):
    slabs = lax.axis_size("depth")
    vmem = pl.BlockSpec(memory_space=pltpu.VMEM)
    smem = pl.BlockSpec(memory_space=pltpu.SMEM)
    return pl.pallas_call(
        functools.partial(kernel, slabs=slabs),
        out_shape=jax.ShapeDtypeStruct((4, 128), F),
        in_specs=[pl.BlockSpec(memory_space=pltpu.HBM), vmem, smem, vmem, vmem, vmem, vmem, vmem, smem],
        out_specs=vmem,
        scratch_shapes=[
            pltpu.VMEM((8, 32, 4, BRICK), BF),
            pltpu.VMEM((2, 2, 256, 256), BF),
            pltpu.VMEM((2, 2, 256, 256), BF),
            pltpu.VMEM((256, 256), BF),
            pltpu.VMEM((2, 16, 256), BF),
            pltpu.VMEM((2, 128, 128), F),
            pltpu.VMEM((2 * 8 * 16, 128), F),
            pltpu.VMEM((2, 256, 256), BF),
            pltpu.VMEM((2, 256, 256), BF),
            pltpu.VMEM((64, 4, 128), F),
            pltpu.VMEM((64, 4, 128), F),
            pltpu.SemaphoreType.DMA((8,)),
            pltpu.SemaphoreType.DMA,
            pltpu.SemaphoreType.DMA,
        ],
        compiler_params=pltpu.CompilerParams(
            collective_id=0, has_side_effects=True, vmem_limit_bytes=60 * 2**20
        ),
    )(
        features,
        ray_spans.reshape(2, 64, 128),
        view_order,
        w_first.T,
        w_second,
        w_last,
        b_first.reshape(1, 128),
        b_second.reshape(1, 128),
        b_last,
    )


def solution(mesh):
    return jax.shard_map(
        per_device,
        mesh=mesh,
        in_specs=(P(None, "depth", "tile"), P(None, "depth", "tile"), P("tile"), P(), P(), P(), P(), P(), P()),
        out_specs=P(None, ("tile", "depth")),
        check_vma=False,
    )
```

```python
import functools

import jax
import jax.numpy as jnp
from jax import lax
from jax.experimental import pallas as pl
from jax.experimental.pallas import tpu as pltpu
from jax.sharding import PartitionSpec as P

BF = jnp.bfloat16
F = jnp.float32
BRICK = 1024
CH = 32
MESH = pl.DeviceIdType.MESH


def over(near, far):
    through = 1.0 - near[3]
    return [a + through * b for a, b in zip(near, far)]


def ordered(flip, first, second):
    near = [jnp.where(flip, b, a) for a, b in zip(first, second)]
    far = [jnp.where(flip, a, b) for a, b in zip(first, second)]
    return over(near, far)


def stack_samples(z_ref, spans, zrow, row, flip, b_last, spacing):
    entry = spans[0, pl.ds(row, 8), :]
    leave = spans[1, pl.ds(row, 8), :]
    remain, opacity = [], []
    for s in range(4):
        density = z_ref[pl.ds(zrow + 4 * s, 8, stride=16), :] + b_last[0]
        soft = jnp.maximum(density, 0.0) + jnp.log1p(jnp.exp(-jnp.abs(density)))
        kept = jnp.exp(soft * (-spacing))
        kept = jnp.where((entry <= s) & (leave > s), kept, 1.0)
        remain.append(kept)
        opacity.append(1.0 - kept)
    p01 = remain[0] * remain[1]
    p012 = p01 * remain[2]
    q32 = remain[3] * remain[2]
    q321 = q32 * remain[1]
    through = [
        jnp.where(flip, q321, 1.0),
        jnp.where(flip, q32, remain[0]),
        jnp.where(flip, remain[3], p01),
        jnp.where(flip, 1.0, p012),
    ]
    weight = [t * o for t, o in zip(through, opacity)]
    layers = []
    for ch in range(3):
        total = None
        for s in range(4):
            color = z_ref[pl.ds(zrow + 4 * s + 1 + ch, 8, stride=16), :] + b_last[1 + ch]
            term = weight[s] * (0.5 * jnp.tanh(0.5 * color) + 0.5)
            total = term if total is None else total + term
        layers.append(total)
    layers.append((weight[0] + weight[1]) + (weight[2] + weight[3]))
    return layers


def kernel(*refs, slabs):
    accs = []
    for m in range(2):
        accs += [pltpu.ACC(m)((CH, 256), F)] * 31 + [pltpu.ACC(m)((16, 256), F)] * 2
    pl.run_scoped(lambda *accs: body(*refs, accs=accs, slabs=slabs), *accs)


def body(
    x_hbm, spans, order, w1t, w2, w3, b1, b2, bl_ref, out,
    xbuf, xs, w1p, w2p, w3p, bias, z_ref, h1s, h2s, sent, taken, sem, send_sem, recv_sem,
    *, accs, slabs,
):
    acc1 = [accs[m * 33 : m * 33 + 16] for m in range(2)]
    acc2 = [accs[m * 33 + 16 : m * 33 + 31] + accs[m * 33 + 16 : m * 33 + 17] for m in range(2)]
    acc3 = [accs[m * 33 + 31 : m * 33 + 33] for m in range(2)]
    bricks = 8
    me = lax.axis_index("depth")
    low = lax.rem(me, 8)
    high = lax.div(me, 8)
    spacing = 6.0 / (4 * slabs)

    def place(k):
        return lax.rem(high + 1 + k, 8)

    def xcopy(k):
        start = pl.multiple_of(place(k) * BRICK, BRICK)
        return pltpu.make_async_copy(x_hbm.at[:, :, pl.ds(start, BRICK)], xbuf.at[k], sem.at[k])

    for k in range(bricks):
        xcopy(k).start()

    barrier = pltpu.get_barrier_semaphore()

    def greet(j, _):
        peer = lax.rem(me + j, slabs)
        pl.semaphore_signal(barrier, inc=1, device_id={"depth": peer}, device_id_type=MESH)
        return 0

    lax.fori_loop(1, slabs, greet, 0)

    first = jnp.concatenate([w1t[...].astype(F), jnp.zeros((96, 128), F)], axis=0)
    first = jnp.transpose(first).astype(BF)
    first = jnp.concatenate([first, jnp.zeros((128, 128), BF)], axis=1)
    channel = lax.broadcasted_iota(jnp.int32, (256, 128), 0)
    column = lax.broadcasted_iota(jnp.int32, (256, 128), 1)
    for q in range(2):
        spread = jnp.concatenate(
            [(column == channel * 4 + (2 * q + k)).astype(F).astype(BF) for k in range(2)], axis=1
        )
        pltpu.matmul_push_rhs(spread, 0, q)
        for i in range(4):
            rows = first[i * CH : (i + 1) * CH]
            pltpu.matmul_acc_lhs(acc1[q][i], rows, load_staged_rhs=0 if i == 0 else None)
    for q in range(2):
        for i in range(4):
            wide = pltpu.matmul_pop(acc1[q][i]).astype(BF)
            for k in range(2):
                rows = pl.ds(q * 256 + k * 128 + i * CH, CH)
                for j in range(2):
                    w1p[j, rows, j * 128 : (j + 1) * 128] = wide[:, k * 128 : (k + 1) * 128]
                    w1p[j, rows, (1 - j) * 128 : (2 - j) * 128] = jnp.zeros((CH, 128), BF)
    for k in range(2):
        w2p[k * 128 : (k + 1) * 128, k * 128 : (k + 1) * 128] = w2[...]
        w2p[k * 128 : (k + 1) * 128, (1 - k) * 128 : (2 - k) * 128] = jnp.zeros((128, 128), BF)
    last = w3[...].astype(F)
    none = jnp.zeros((4, 128), F)
    for q in range(2):
        left = jnp.concatenate([last if s == 2 * q else none for s in range(4)], axis=0)
        right = jnp.concatenate([last if s == 2 * q + 1 else none for s in range(4)], axis=0)
        w3p[q] = jnp.concatenate([left, right], axis=1).astype(BF)
    bias[0] = jnp.transpose(jnp.broadcast_to(b1[...], (128, 128)))
    bias[1] = jnp.transpose(jnp.broadcast_to(b2[...], (128, 128)))
    flip = jnp.full((8, 128), order[0], jnp.int32) == 1
    b_last = [bl_ref[i] for i in range(4)]

    def prep(k):
        for m in range(2):
            for j in range(2):
                tile = xbuf[k, :, :, m * 512 + j * 256 : m * 512 + (j + 1) * 256]
                xs[lax.rem(k, 2), m, j * 128 : (j + 1) * 128, :] = tile.reshape(128, 256)

    def push(source, stage):
        for m in range(2):
            pltpu.matmul_push_rhs(source(m), stage, m)

    def mm1(j, i, stage):
        for m in range(2):
            rows = w1p[j, i * CH : (i + 1) * CH, :]
            pltpu.matmul_acc_lhs(acc1[m][i], rows, load_staged_rhs=stage if i == 0 else None)

    def mm2(i, stage):
        for m in range(2):
            rows = w2p[(i % 8) * CH : (i % 8 + 1) * CH, :]
            pltpu.matmul_acc_lhs(acc2[m][i], rows, load_staged_rhs=stage if i % 8 == 0 else None)

    def mm3(j, q, stage):
        for m in range(2):
            pltpu.matmul_acc_lhs(acc3[m][j], w3p[q], load_staged_rhs=stage)

    def settle(acc, layer, i, dst):
        r = (i * CH) % 128
        shift = bias[layer, r : r + CH, :]
        shift = jnp.concatenate([shift, shift], axis=1)
        for m in range(2):
            value = (pltpu.matmul_pop(acc[m][i]) + shift).astype(BF)
            dst[m, i * CH : (i + 1) * CH, :] = jnp.maximum(value, jnp.zeros((), BF))

    def pop3(j, par):
        for m in range(2):
            value = pltpu.matmul_pop(acc3[m][j])
            row = par * 128 + 32 * (2 * m + j)
            z_ref[pl.ds(row, 16), :] = value[:, :128]
            z_ref[pl.ds(row + 16, 16), :] = value[:, 128:]

    def slot(k, j, first=False, second=False, last=False, last_brick=False, middle=None, late=None):
        par = lax.rem(k, 2)
        s0, s1 = j % 2, 1 - j % 2
        push(lambda m: h1s[m, 0:256, :], s1)
        for i in range(16):
            if not last:
                mm1(1 - j, i, s0)
            if i >= 1 and not first:
                settle(acc2, 1, i, h2s)
            if i == 8 and not first:
                push(lambda m: h2s[m, 0:256, :], s0)
        if middle:
            middle()
        if not first and not second:
            pop3(j, 1 - par)
        for i in range(8):
            mm2(i, s1)
            if not last:
                settle(acc1, 0, i, h1s)
        push(lambda m: h1s[m, 256:512, :], s1)
        if not first:
            mm3(1 - j, 0, s0)
            push(lambda m: h2s[m, 256:512, :], s0)
        for i in range(8, 16):
            if i == 15:
                settle(acc2, 1, 0, h2s)
            mm2(i, s1)
            if not last:
                settle(acc1, 0, i, h1s)
        if late:
            late()
        if not last_brick:
            push(lambda m: xs[1 - par, m], s1)
        if not first:
            mm3(1 - j, 1, s0)

    def brick(k, first=False, last=False, late=None):
        if not last:
            xcopy(k + 1).wait()
        middle = None if last else lambda: prep(k + 1)
        slot(k, 0, first=first, last_brick=last, middle=middle)
        slot(k, 1, second=first, last=last, last_brick=last, late=late)

    def send(k, j):
        chunk = lax.rem(low + j, 8)
        return pltpu.make_async_remote_copy(
            src_ref=sent.at[k * 8 + chunk],
            dst_ref=taken.at[me],
            send_sem=send_sem,
            recv_sem=recv_sem,
            device_id={"depth": place(k) * 8 + chunk},
            device_id_type=MESH,
        )

    def finish(k):
        row = pl.multiple_of(place(k) * 8, 8)
        layers = stack_samples(z_ref, spans, lax.rem(k, 2) * 128, row, flip, b_last, spacing)
        for ch in range(4):
            sent[pl.ds(k * 8, 8), ch, :] = layers[ch]

    def finish_send(k):
        finish(k)
        for j in range(8):
            send(k, j).start()

    xcopy(0).wait()
    prep(0)
    push(lambda m: xs[0, m], 1)
    for i in range(16):
        mm1(0, i, 1)
    push(lambda m: xs[0, m], 0)
    for i in range(16):
        settle(acc1, 0, i, h1s)
    brick(0, first=True)
    pl.semaphore_wait(barrier, slabs - 1)

    def step(k, _):
        brick(k, late=lambda: finish_send(k - 1))
        return 0

    lax.fori_loop(1, bricks - 1, step, 0)
    brick(bricks - 1, last=True, late=lambda: finish_send(bricks - 2))
    for i in range(1, 16):
        settle(acc2, 1, i, h2s)
    push(lambda m: h2s[m, 0:256, :], 0)
    push(lambda m: h2s[m, 256:512, :], 1)
    pop3(0, (bricks - 1) % 2)
    mm3(1, 0, 0)
    mm3(1, 1, 1)
    pop3(1, (bricks - 1) % 2)
    finish(bricks - 1)
    for j in range(1, 8):
        send(bricks - 1, j).start()
    taken[me] = sent[(bricks - 1) * 8 + low]

    others = pltpu.make_async_remote_copy(
        src_ref=sent.at[pl.ds(0, slabs - 1)],
        dst_ref=taken.at[pl.ds(0, slabs - 1)],
        send_sem=send_sem,
        recv_sem=recv_sem,
        device_id={"depth": lax.rem(me + 1, slabs)},
        device_id_type=MESH,
    )
    others.wait_recv()
    groups = [[taken[pl.ds(k, 8, stride=8), ch, :] for ch in range(4)] for k in range(8)]
    while len(groups) > 1:
        groups = [ordered(flip, a, b) for a, b in zip(groups[::2], groups[1::2])]
    total = groups[0]
    for shift in (7, 6, 4):
        total = ordered(flip, total, [pltpu.roll(c, shift, 0) for c in total])
    out[...] = jnp.concatenate([c[0:1] for c in total], axis=0)
    others.wait_send()


def per_device(features, ray_spans, view_order, w_first, b_first, w_second, b_second, w_last, b_last):
    slabs = lax.axis_size("depth")
    vmem = pl.BlockSpec(memory_space=pltpu.VMEM)
    smem = pl.BlockSpec(memory_space=pltpu.SMEM)
    return pl.pallas_call(
        functools.partial(kernel, slabs=slabs),
        out_shape=jax.ShapeDtypeStruct((4, 128), F),
        in_specs=[pl.BlockSpec(memory_space=pltpu.HBM), vmem, smem, vmem, vmem, vmem, vmem, vmem, smem],
        out_specs=vmem,
        scratch_shapes=[
            pltpu.VMEM((8, 32, 4, BRICK), BF),
            pltpu.VMEM((2, 2, 256, 256), BF),
            pltpu.VMEM((2, 512, 256), BF),
            pltpu.VMEM((256, 256), BF),
            pltpu.VMEM((2, 16, 256), BF),
            pltpu.VMEM((2, 128, 128), F),
            pltpu.VMEM((2 * 8 * 16, 128), F),
            pltpu.VMEM((2, 512, 256), BF),
            pltpu.VMEM((2, 512, 256), BF),
            pltpu.VMEM((64, 4, 128), F),
            pltpu.VMEM((64, 4, 128), F),
            pltpu.SemaphoreType.DMA((8,)),
            pltpu.SemaphoreType.DMA,
            pltpu.SemaphoreType.DMA,
        ],
        compiler_params=pltpu.CompilerParams(
            collective_id=0, has_side_effects=True, vmem_limit_bytes=60 * 2**20
        ),
    )(
        features,
        ray_spans.reshape(2, 64, 128),
        view_order,
        w_first.T,
        w_second,
        w_last,
        b_first.reshape(1, 128),
        b_second.reshape(1, 128),
        b_last,
    )


def solution(mesh):
    return jax.shard_map(
        per_device,
        mesh=mesh,
        in_specs=(P(None, "depth", "tile"), P(None, "depth", "tile"), P("tile"), P(), P(), P(), P(), P(), P()),
        out_specs=P(None, ("tile", "depth")),
        check_vma=False,
    )
```

```python
import functools

import jax
import jax.numpy as jnp
from jax import lax
from jax.experimental import pallas as pl
from jax.experimental.pallas import tpu as pltpu
from jax.sharding import PartitionSpec as P

BF = jnp.bfloat16
F = jnp.float32
BRICK = 1024
CH = 32
MESH = pl.DeviceIdType.MESH
AWAY = (4, 3, 5, 2, 6, 1, 7, 0)
PEERS = sorted(
    ((a, b) for a in range(8) for b in range(8) if a or b),
    key=lambda p: -(min(p[0], 8 - p[0]) + min(p[1], 8 - p[1])),
)


def over(near, far):
    through = 1.0 - near[3]
    return [a + through * b for a, b in zip(near, far)]


def ordered(flip, first, second):
    near = [jnp.where(flip, b, a) for a, b in zip(first, second)]
    far = [jnp.where(flip, a, b) for a, b in zip(first, second)]
    return over(near, far)


def stack_samples(z_ref, spans, zrow, row, flip, b_last, spacing):
    entry = spans[0, pl.ds(row, 8), :]
    leave = spans[1, pl.ds(row, 8), :]
    remain, opacity = [], []
    for s in range(4):
        density = z_ref[pl.ds(zrow + 4 * s, 8, stride=16), :] + b_last[0]
        soft = jnp.maximum(density, 0.0) + jnp.log1p(jnp.exp(-jnp.abs(density)))
        kept = jnp.exp(soft * (-spacing))
        kept = jnp.where((entry <= s) & (leave > s), kept, 1.0)
        remain.append(kept)
        opacity.append(1.0 - kept)
    p01 = remain[0] * remain[1]
    p012 = p01 * remain[2]
    q32 = remain[3] * remain[2]
    q321 = q32 * remain[1]
    through = [
        jnp.where(flip, q321, 1.0),
        jnp.where(flip, q32, remain[0]),
        jnp.where(flip, remain[3], p01),
        jnp.where(flip, 1.0, p012),
    ]
    weight = [t * o for t, o in zip(through, opacity)]
    layers = []
    for ch in range(3):
        total = None
        for s in range(4):
            color = z_ref[pl.ds(zrow + 4 * s + 1 + ch, 8, stride=16), :] + b_last[1 + ch]
            term = weight[s] * (0.5 * jnp.tanh(0.5 * color) + 0.5)
            total = term if total is None else total + term
        layers.append(total)
    layers.append((weight[0] + weight[1]) + (weight[2] + weight[3]))
    return layers


def kernel(*refs, slabs):
    accs = []
    for m in range(2):
        accs += [pltpu.ACC(m)((CH, 256), F)] * 31 + [pltpu.ACC(m)((16, 256), F)] * 2
    pl.run_scoped(lambda *accs: body(*refs, accs=accs, slabs=slabs), *accs)


def body(
    x_hbm, spans_hbm, order, w1_hbm, w2_hbm, w3_hbm, b1_hbm, b2_hbm, bl_hbm, out,
    xbuf, xs, w1p, w2p, w3p, bias, z_ref, h1s, h2s, sent, taken,
    spans, w1t, w2, w3, b1, b2, bl, sem, small_sem, send_sem, recv_sem,
    *, accs, slabs,
):
    acc1 = [accs[m * 33 : m * 33 + 16] for m in range(2)]
    acc2 = [accs[m * 33 + 16 : m * 33 + 31] + accs[m * 33 + 16 : m * 33 + 17] for m in range(2)]
    acc3 = [accs[m * 33 + 31 : m * 33 + 33] for m in range(2)]
    bricks = 8
    me = lax.axis_index("depth")
    low = lax.rem(me, 8)
    high = lax.div(me, 8)
    spacing = 6.0 / (4 * slabs)

    barrier = pltpu.get_barrier_semaphore()
    for dx, dz in PEERS:
        peer = lax.rem(high + dx, 8) * 8 + lax.rem(low + dz, 8)
        pl.semaphore_signal(barrier, inc=1, device_id={"depth": peer}, device_id_type=MESH)

    def place(k):
        step = lax.div(k + 1, 2)
        away = jnp.where(lax.rem(k, 2) == 1, 4 - step, 4 + step)
        return lax.rem(high + lax.rem(away, 8), 8)

    def xcopy(k):
        start = pl.multiple_of(place(k) * BRICK, BRICK)
        return pltpu.make_async_copy(x_hbm.at[:, :, pl.ds(start, BRICK)], xbuf.at[k], sem.at[k])

    small = [
        pltpu.make_async_copy(src, dst, small_sem.at[i])
        for i, (src, dst) in enumerate(
            (
                (w1_hbm, w1t), (w2_hbm, w2), (w3_hbm, w3), (b1_hbm, b1), (b2_hbm, b2),
                (bl_hbm, bl), (spans_hbm, spans),
            )
        )
    ]
    for copy in small[:1]:
        copy.start()
    xcopy(0).start()
    for copy in small[1:]:
        copy.start()
    for k in range(1, bricks):
        xcopy(k).start()
    for copy in small:
        copy.wait()

    first = jnp.concatenate([w1t[...].astype(F), jnp.zeros((96, 128), F)], axis=0)
    first = jnp.transpose(first).astype(BF)
    first = jnp.concatenate([first, jnp.zeros((128, 128), BF)], axis=1)
    channel = lax.broadcasted_iota(jnp.int32, (256, 128), 0)
    column = lax.broadcasted_iota(jnp.int32, (256, 128), 1)
    for q in range(2):
        spread = jnp.concatenate(
            [(column == channel * 4 + (2 * q + k)).astype(F).astype(BF) for k in range(2)], axis=1
        )
        pltpu.matmul_push_rhs(spread, 0, q)
        for i in range(4):
            rows = first[i * CH : (i + 1) * CH]
            pltpu.matmul_acc_lhs(acc1[q][i], rows, load_staged_rhs=0 if i == 0 else None)
    for q in range(2):
        for i in range(4):
            wide = pltpu.matmul_pop(acc1[q][i]).astype(BF)
            for k in range(2):
                rows = pl.ds(q * 256 + k * 128 + i * CH, CH)
                for j in range(2):
                    w1p[j, rows, j * 128 : (j + 1) * 128] = wide[:, k * 128 : (k + 1) * 128]
                    w1p[j, rows, (1 - j) * 128 : (2 - j) * 128] = jnp.zeros((CH, 128), BF)
    for k in range(2):
        w2p[k * 128 : (k + 1) * 128, k * 128 : (k + 1) * 128] = w2[...]
        w2p[k * 128 : (k + 1) * 128, (1 - k) * 128 : (2 - k) * 128] = jnp.zeros((128, 128), BF)
    last = w3[...].astype(F)
    none = jnp.zeros((4, 128), F)
    for q in range(2):
        left = jnp.concatenate([last if s == 2 * q else none for s in range(4)], axis=0)
        right = jnp.concatenate([last if s == 2 * q + 1 else none for s in range(4)], axis=0)
        w3p[q] = jnp.concatenate([left, right], axis=1).astype(BF)
    bias[0] = jnp.transpose(jnp.broadcast_to(b1[...], (128, 128)))
    bias[1] = jnp.transpose(jnp.broadcast_to(b2[...], (128, 128)))
    flip = jnp.full((8, 128), order[0], jnp.int32) == 1
    b_last = [jnp.broadcast_to(bl[0:1, i : i + 1], (8, 128)) for i in range(4)]

    def prep(k):
        for m in range(2):
            for j in range(2):
                tile = xbuf[k, :, :, m * 512 + j * 256 : m * 512 + (j + 1) * 256]
                xs[lax.rem(k, 2), m, j * 128 : (j + 1) * 128, :] = tile.reshape(128, 256)

    def push(source, stage):
        for m in range(2):
            pltpu.matmul_push_rhs(source(m), stage, m)

    def mm1(j, i, stage):
        for m in range(2):
            rows = w1p[j, i * CH : (i + 1) * CH, :]
            pltpu.matmul_acc_lhs(acc1[m][i], rows, load_staged_rhs=stage if i == 0 else None)

    def mm2(i, stage):
        for m in range(2):
            rows = w2p[(i % 8) * CH : (i % 8 + 1) * CH, :]
            pltpu.matmul_acc_lhs(acc2[m][i], rows, load_staged_rhs=stage if i % 8 == 0 else None)

    def mm3(j, q, stage):
        for m in range(2):
            pltpu.matmul_acc_lhs(acc3[m][j], w3p[q], load_staged_rhs=stage)

    def settle(acc, layer, i, dst):
        r = (i * CH) % 128
        shift = bias[layer, r : r + CH, :]
        shift = jnp.concatenate([shift, shift], axis=1)
        for m in range(2):
            value = (pltpu.matmul_pop(acc[m][i]) + shift).astype(BF)
            dst[m, i * CH : (i + 1) * CH, :] = jnp.maximum(value, jnp.zeros((), BF))

    def pop3(j, par):
        for m in range(2):
            value = pltpu.matmul_pop(acc3[m][j])
            row = par * 128 + 32 * (2 * m + j)
            z_ref[pl.ds(row, 16), :] = value[:, :128]
            z_ref[pl.ds(row + 16, 16), :] = value[:, 128:]

    def slot(k, j, first=False, second=False, last=False, last_brick=False, middle=None, late=None):
        par = lax.rem(k, 2)
        s0, s1 = j % 2, 1 - j % 2
        push(lambda m: h1s[m, 0:256, :], s1)
        for i in range(16):
            if not last:
                mm1(1 - j, i, s0)
            if i >= 1 and not first:
                settle(acc2, 1, i, h2s)
            if i == 8 and not first:
                push(lambda m: h2s[m, 0:256, :], s0)
        if middle:
            middle()
        if not first and not second:
            pop3(j, 1 - par)
        for i in range(8):
            mm2(i, s1)
            if not last:
                settle(acc1, 0, i, h1s)
        push(lambda m: h1s[m, 256:512, :], s1)
        if not first:
            mm3(1 - j, 0, s0)
            push(lambda m: h2s[m, 256:512, :], s0)
        for i in range(8, 16):
            if i == 15:
                settle(acc2, 1, 0, h2s)
            mm2(i, s1)
            if not last:
                settle(acc1, 0, i, h1s)
        if late:
            late()
        if not last_brick:
            push(lambda m: xs[1 - par, m], s1)
        if not first:
            mm3(1 - j, 1, s0)

    def brick(k, first=False, last=False, late=None):
        if not last:
            xcopy(k + 1).wait()
        middle = None if last else lambda: prep(k + 1)
        slot(k, 0, first=first, last_brick=last, middle=middle)
        slot(k, 1, second=first, last=last, last_brick=last, late=late)

    def send(k, j):
        chunk = lax.rem(low + AWAY[j], 8)
        return pltpu.make_async_remote_copy(
            src_ref=sent.at[k * 8 + chunk],
            dst_ref=taken.at[me],
            send_sem=send_sem,
            recv_sem=recv_sem,
            device_id={"depth": place(k) * 8 + chunk},
            device_id_type=MESH,
        )

    def finish(k):
        row = pl.multiple_of(place(k) * 8, 8)
        layers = stack_samples(z_ref, spans, lax.rem(k, 2) * 128, row, flip, b_last, spacing)
        for ch in range(4):
            sent[pl.ds(k * 8, 8), ch, :] = layers[ch]

    def send_brick(k):
        for j in range(8):
            send(k, j).start()

    xcopy(0).wait()
    prep(0)
    push(lambda m: xs[0, m], 1)
    for i in range(16):
        mm1(0, i, 1)
    push(lambda m: xs[0, m], 0)
    for i in range(16):
        settle(acc1, 0, i, h1s)
    brick(0, first=True)

    def step(k, _):
        brick(k, late=lambda: finish(k - 1))

        @pl.when(k == 2)
        def _():
            pl.semaphore_wait(barrier, slabs - 1)
            send_brick(0)

        @pl.when(k >= 2)
        def _():
            send_brick(k - 1)

        return 0

    lax.fori_loop(1, bricks - 1, step, 0)
    brick(bricks - 1, last=True, late=lambda: finish(bricks - 2))
    send_brick(bricks - 2)
    for i in range(1, 16):
        settle(acc2, 1, i, h2s)
    push(lambda m: h2s[m, 0:256, :], 0)
    push(lambda m: h2s[m, 256:512, :], 1)
    pop3(0, (bricks - 1) % 2)
    mm3(1, 0, 0)
    mm3(1, 1, 1)
    pop3(1, (bricks - 1) % 2)
    finish(bricks - 1)
    for j in range(7):
        send(bricks - 1, j).start()
    taken[me] = sent[(bricks - 1) * 8 + low]

    others = pltpu.make_async_remote_copy(
        src_ref=sent.at[pl.ds(0, slabs - 1)],
        dst_ref=taken.at[pl.ds(0, slabs - 1)],
        send_sem=send_sem,
        recv_sem=recv_sem,
        device_id={"depth": lax.rem(me + 1, slabs)},
        device_id_type=MESH,
    )
    others.wait_recv()
    groups = [[taken[pl.ds(k, 8, stride=8), ch, :] for ch in range(4)] for k in range(8)]
    while len(groups) > 1:
        groups = [ordered(flip, a, b) for a, b in zip(groups[::2], groups[1::2])]
    total = groups[0]
    for shift in (7, 6, 4):
        total = ordered(flip, total, [pltpu.roll(c, shift, 0) for c in total])
    out[...] = jnp.concatenate([c[0:1] for c in total], axis=0)
    others.wait_send()


def per_device(features, ray_spans, view_order, w_first, b_first, w_second, b_second, w_last, b_last):
    slabs = lax.axis_size("depth")
    hbm = pl.BlockSpec(memory_space=pltpu.HBM)
    return pl.pallas_call(
        functools.partial(kernel, slabs=slabs),
        out_shape=jax.ShapeDtypeStruct((4, 128), F),
        in_specs=[hbm, hbm, pl.BlockSpec(memory_space=pltpu.SMEM)] + [hbm] * 6,
        out_specs=pl.BlockSpec(memory_space=pltpu.VMEM),
        scratch_shapes=[
            pltpu.VMEM((8, 32, 4, BRICK), BF),
            pltpu.VMEM((2, 2, 256, 256), BF),
            pltpu.VMEM((2, 512, 256), BF),
            pltpu.VMEM((256, 256), BF),
            pltpu.VMEM((2, 16, 256), BF),
            pltpu.VMEM((2, 128, 128), F),
            pltpu.VMEM((2 * 8 * 16, 128), F),
            pltpu.VMEM((2, 512, 256), BF),
            pltpu.VMEM((2, 512, 256), BF),
            pltpu.VMEM((64, 4, 128), F),
            pltpu.VMEM((64, 4, 128), F),
            pltpu.VMEM((2, 64, 128), jnp.int32),
            pltpu.VMEM((32, 128), BF),
            pltpu.VMEM((128, 128), BF),
            pltpu.VMEM((4, 128), BF),
            pltpu.VMEM((1, 128), F),
            pltpu.VMEM((1, 128), F),
            pltpu.VMEM((1, 4), F),
            pltpu.SemaphoreType.DMA((8,)),
            pltpu.SemaphoreType.DMA((7,)),
            pltpu.SemaphoreType.DMA,
            pltpu.SemaphoreType.DMA,
        ],
        compiler_params=pltpu.CompilerParams(
            collective_id=0, has_side_effects=True, vmem_limit_bytes=60 * 2**20
        ),
    )(
        features,
        ray_spans.reshape(2, 64, 128),
        view_order,
        w_first.T,
        w_second,
        w_last,
        b_first.reshape(1, 128),
        b_second.reshape(1, 128),
        b_last.reshape(1, 4),
    )


def solution(mesh):
    return jax.shard_map(
        per_device,
        mesh=mesh,
        in_specs=(P(None, "depth", "tile"), P(None, "depth", "tile"), P("tile"), P(), P(), P(), P(), P(), P()),
        out_specs=P(None, ("tile", "depth")),
        check_vma=False,
    )
```

```python
import functools

import jax
import jax.numpy as jnp
from jax import lax
from jax.experimental import pallas as pl
from jax.experimental.pallas import tpu as pltpu
from jax.sharding import PartitionSpec as P

BF = jnp.bfloat16
F = jnp.float32
BRICK = 1024
CH = 32
MESH = pl.DeviceIdType.MESH
AWAY = (4, 3, 5, 2, 6, 1, 7, 0)
PEERS = sorted(
    ((a, b) for a in range(8) for b in range(8) if a or b),
    key=lambda p: -(min(p[0], 8 - p[0]) + min(p[1], 8 - p[1])),
)


def over(near, far):
    through = 1.0 - near[3]
    return [a + through * b for a, b in zip(near, far)]


def ordered(flip, first, second):
    near = [jnp.where(flip, b, a) for a, b in zip(first, second)]
    far = [jnp.where(flip, a, b) for a, b in zip(first, second)]
    return over(near, far)


def stack_samples(z_ref, spans, zrow, row, flip, b_last, spacing):
    entry = spans[0, pl.ds(row, 8), :]
    leave = spans[1, pl.ds(row, 8), :]
    remain, opacity = [], []
    for s in range(4):
        density = z_ref[pl.ds(zrow + 4 * s, 8, stride=16), :] + b_last[0]
        soft = jnp.maximum(density, 0.0) + jnp.log1p(jnp.exp(-jnp.abs(density)))
        kept = jnp.exp(soft * (-spacing))
        kept = jnp.where((entry <= s) & (leave > s), kept, 1.0)
        remain.append(kept)
        opacity.append(1.0 - kept)
    p01 = remain[0] * remain[1]
    p012 = p01 * remain[2]
    q32 = remain[3] * remain[2]
    q321 = q32 * remain[1]
    through = [
        jnp.where(flip, q321, 1.0),
        jnp.where(flip, q32, remain[0]),
        jnp.where(flip, remain[3], p01),
        jnp.where(flip, 1.0, p012),
    ]
    weight = [t * o for t, o in zip(through, opacity)]
    layers = []
    for ch in range(3):
        total = None
        for s in range(4):
            color = z_ref[pl.ds(zrow + 4 * s + 1 + ch, 8, stride=16), :] + b_last[1 + ch]
            term = weight[s] * (0.5 * jnp.tanh(0.5 * color) + 0.5)
            total = term if total is None else total + term
        layers.append(total)
    layers.append((weight[0] + weight[1]) + (weight[2] + weight[3]))
    return layers


def kernel(*refs, slabs):
    accs = []
    for m in range(2):
        accs += [pltpu.ACC(m)((CH, 256), F)] * 31 + [pltpu.ACC(m)((16, 256), F)] * 2
    pl.run_scoped(lambda *accs: body(*refs, accs=accs, slabs=slabs), *accs)


def body(
    x_hbm, spans_hbm, order, w1_hbm, w2_hbm, w3_hbm, b1_hbm, b2_hbm, bl_hbm, out,
    xbuf, xs, w1p, w2p, w3p, bias, z_ref, h1s, h2s, sent, taken,
    spans, w1t, w2, w3, b1, b2, bl, sem, small_sem, send_sem, recv_sem,
    *, accs, slabs,
):
    acc1 = [accs[m * 33 : m * 33 + 16] for m in range(2)]
    acc2 = [accs[m * 33 + 16 : m * 33 + 31] + accs[m * 33 + 16 : m * 33 + 17] for m in range(2)]
    acc3 = [accs[m * 33 + 31 : m * 33 + 33] for m in range(2)]
    bricks = 8
    me = lax.axis_index("depth")
    low = lax.rem(me, 8)
    high = lax.div(me, 8)
    spacing = 6.0 / (4 * slabs)

    barrier = pltpu.get_barrier_semaphore()
    for dx, dz in PEERS:
        peer = lax.rem(high + dx, 8) * 8 + lax.rem(low + dz, 8)
        pl.semaphore_signal(barrier, inc=1, device_id={"depth": peer}, device_id_type=MESH)

    def place(k):
        step = lax.div(k + 1, 2)
        away = jnp.where(lax.rem(k, 2) == 1, 4 - step, 4 + step)
        return lax.rem(high + lax.rem(away, 8), 8)

    def xcopy(k):
        start = pl.multiple_of(place(k) * BRICK, BRICK)
        return pltpu.make_async_copy(x_hbm.at[:, :, pl.ds(start, BRICK)], xbuf.at[k], sem.at[k])

    small = [
        pltpu.make_async_copy(src, dst, small_sem.at[i])
        for i, (src, dst) in enumerate(
            (
                (w1_hbm, w1t), (w2_hbm, w2), (w3_hbm, w3), (b1_hbm, b1), (b2_hbm, b2),
                (bl_hbm, bl), (spans_hbm, spans),
            )
        )
    ]
    for copy in small[:1]:
        copy.start()
    xcopy(0).start()
    for copy in small[1:]:
        copy.start()
    for k in range(1, bricks):
        xcopy(k).start()
    for copy in small:
        copy.wait()

    first = jnp.concatenate([w1t[...].astype(F), jnp.zeros((96, 128), F)], axis=0)
    first = jnp.transpose(first).astype(BF)
    first = jnp.concatenate([first, jnp.zeros((128, 128), BF)], axis=1)
    channel = lax.broadcasted_iota(jnp.int32, (256, 128), 0)
    column = lax.broadcasted_iota(jnp.int32, (256, 128), 1)
    for q in range(2):
        spread = jnp.concatenate(
            [(column == channel * 4 + (2 * q + k)).astype(F).astype(BF) for k in range(2)], axis=1
        )
        pltpu.matmul_push_rhs(spread, 0, q)
        for i in range(4):
            rows = first[i * CH : (i + 1) * CH]
            pltpu.matmul_acc_lhs(acc1[q][i], rows, load_staged_rhs=0 if i == 0 else None)
    for q in range(2):
        for i in range(4):
            wide = pltpu.matmul_pop(acc1[q][i]).astype(BF)
            for k in range(2):
                rows = pl.ds(q * 256 + k * 128 + i * CH, CH)
                for j in range(2):
                    w1p[j, rows, j * 128 : (j + 1) * 128] = wide[:, k * 128 : (k + 1) * 128]
                    w1p[j, rows, (1 - j) * 128 : (2 - j) * 128] = jnp.zeros((CH, 128), BF)
    for k in range(2):
        w2p[k * 128 : (k + 1) * 128, k * 128 : (k + 1) * 128] = w2[...]
        w2p[k * 128 : (k + 1) * 128, (1 - k) * 128 : (2 - k) * 128] = jnp.zeros((128, 128), BF)
    last = w3[...].astype(F)
    none = jnp.zeros((4, 128), F)
    for q in range(2):
        left = jnp.concatenate([last if s == 2 * q else none for s in range(4)], axis=0)
        right = jnp.concatenate([last if s == 2 * q + 1 else none for s in range(4)], axis=0)
        w3p[q] = jnp.concatenate([left, right], axis=1).astype(BF)
    bias[0] = jnp.transpose(jnp.broadcast_to(b1[...], (128, 128)))
    bias[1] = jnp.transpose(jnp.broadcast_to(b2[...], (128, 128)))
    flip = jnp.full((8, 128), order[0], jnp.int32) == 1
    b_last = [jnp.broadcast_to(bl[0:1, i : i + 1], (8, 128)) for i in range(4)]

    def prep(k):
        for m in range(2):
            for j in range(2):
                tile = xbuf[k, :, :, m * 512 + j * 256 : m * 512 + (j + 1) * 256]
                xs[lax.rem(k, 2), m, j * 128 : (j + 1) * 128, :] = tile.reshape(128, 256)

    def push(source, stage):
        for m in range(2):
            pltpu.matmul_push_rhs(source(m), stage, m)

    def mm1(j, i, stage):
        for m in range(2):
            rows = w1p[j, i * CH : (i + 1) * CH, :]
            pltpu.matmul_acc_lhs(acc1[m][i], rows, load_staged_rhs=stage if i == 0 else None)

    def mm2(i, stage):
        for m in range(2):
            rows = w2p[(i % 8) * CH : (i % 8 + 1) * CH, :]
            pltpu.matmul_acc_lhs(acc2[m][i], rows, load_staged_rhs=stage if i % 8 == 0 else None)

    def mm3(j, q, stage):
        for m in range(2):
            pltpu.matmul_acc_lhs(acc3[m][j], w3p[q], load_staged_rhs=stage)

    def settle(acc, layer, i, dst):
        r = (i * CH) % 128
        shift = bias[layer, r : r + CH, :]
        shift = jnp.concatenate([shift, shift], axis=1)
        for m in range(2):
            value = (pltpu.matmul_pop(acc[m][i]) + shift).astype(BF)
            dst[m, i * CH : (i + 1) * CH, :] = jnp.maximum(value, jnp.zeros((), BF))

    def pop3(j, par):
        for m in range(2):
            value = pltpu.matmul_pop(acc3[m][j])
            row = par * 128 + 32 * (2 * m + j)
            z_ref[pl.ds(row, 16), :] = value[:, :128]
            z_ref[pl.ds(row + 16, 16), :] = value[:, 128:]

    def slot(k, j, first=False, second=False, last=False, last_brick=False, middle=None, late=None):
        par = lax.rem(k, 2)
        s0, s1 = j % 2, 1 - j % 2
        push(lambda m: h1s[m, 0:256, :], s1)
        for i in range(16):
            if not last:
                mm1(1 - j, i, s0)
            if i >= 1 and not first:
                settle(acc2, 1, i, h2s)
            if i == 8 and not first:
                push(lambda m: h2s[m, 0:256, :], s0)
        if middle:
            middle()
        if not first and not second:
            pop3(j, 1 - par)
        for i in range(8):
            mm2(i, s1)
            if not last:
                settle(acc1, 0, i, h1s)
        push(lambda m: h1s[m, 256:512, :], s1)
        if not first:
            mm3(1 - j, 0, s0)
            push(lambda m: h2s[m, 256:512, :], s0)
        for i in range(8, 16):
            if i == 15:
                settle(acc2, 1, 0, h2s)
            mm2(i, s1)
            if not last:
                settle(acc1, 0, i, h1s)
        if late:
            late()
        if not last_brick:
            push(lambda m: xs[1 - par, m], s1)
        if not first:
            mm3(1 - j, 1, s0)

    def brick(k, first=False, last=False, late=None):
        if not last:
            xcopy(k + 1).wait()
        middle = None if last else lambda: prep(k + 1)
        slot(k, 0, first=first, last_brick=last, middle=middle)
        slot(k, 1, second=first, last=last, last_brick=last, late=late)

    def send(k, j):
        chunk = lax.rem(low + AWAY[j], 8)
        return pltpu.make_async_remote_copy(
            src_ref=sent.at[k * 8 + chunk],
            dst_ref=taken.at[me],
            send_sem=send_sem,
            recv_sem=recv_sem,
            device_id={"depth": place(k) * 8 + chunk},
            device_id_type=MESH,
        )

    def finish(k):
        row = pl.multiple_of(place(k) * 8, 8)
        layers = stack_samples(z_ref, spans, lax.rem(k, 2) * 128, row, flip, b_last, spacing)
        for ch in range(4):
            sent[pl.ds(k * 8, 8), ch, :] = layers[ch]

    def send_brick(k):
        for j in range(8):
            send(k, j).start()

    xcopy(0).wait()
    prep(0)
    push(lambda m: xs[0, m], 1)
    for i in range(16):
        mm1(0, i, 1)
    push(lambda m: xs[0, m], 0)
    for i in range(16):
        settle(acc1, 0, i, h1s)
    brick(0, first=True)

    def step(k, _):
        brick(k, late=lambda: finish(k - 1))

        @pl.when(k == 2)
        def _():
            pl.semaphore_wait(barrier, slabs - 1)
            send_brick(0)

        @pl.when(k >= 2)
        def _():
            send_brick(k - 1)

        return 0

    lax.fori_loop(1, bricks - 1, step, 0)
    brick(bricks - 1, last=True, late=lambda: finish(bricks - 2))
    send_brick(bricks - 2)
    for i in range(1, 16):
        settle(acc2, 1, i, h2s)
    push(lambda m: h2s[m, 0:256, :], 0)
    push(lambda m: h2s[m, 256:512, :], 1)
    pop3(0, (bricks - 1) % 2)
    mm3(1, 0, 0)
    mm3(1, 1, 1)
    pop3(1, (bricks - 1) % 2)
    finish(bricks - 1)
    for j in range(7):
        send(bricks - 1, j).start()
    taken[me] = sent[(bricks - 1) * 8 + low]

    others = pltpu.make_async_remote_copy(
        src_ref=sent.at[pl.ds(0, slabs - 1)],
        dst_ref=taken.at[pl.ds(0, slabs - 1)],
        send_sem=send_sem,
        recv_sem=recv_sem,
        device_id={"depth": lax.rem(me + 1, slabs)},
        device_id_type=MESH,
    )
    others.wait_recv()
    groups = [[taken[pl.ds(k, 8, stride=8), ch, :] for ch in range(4)] for k in range(8)]
    while len(groups) > 1:
        groups = [ordered(flip, a, b) for a, b in zip(groups[::2], groups[1::2])]
    total = groups[0]
    for shift in (7, 6, 4):
        total = ordered(flip, total, [pltpu.roll(c, shift, 0) for c in total])
    out[...] = jnp.concatenate([c[0:1] for c in total], axis=0)
    others.wait_send()


def per_device(features, ray_spans, view_order, w_first, b_first, w_second, b_second, w_last, b_last):
    slabs = lax.axis_size("depth")
    hbm = pl.BlockSpec(memory_space=pltpu.HBM)
    return pl.pallas_call(
        functools.partial(kernel, slabs=slabs),
        out_shape=jax.ShapeDtypeStruct((4, 128), F),
        in_specs=[hbm, hbm, pl.BlockSpec(memory_space=pltpu.SMEM)] + [hbm] * 6,
        out_specs=pl.BlockSpec(memory_space=pltpu.VMEM),
        scratch_shapes=[
            pltpu.VMEM((8, 32, 4, BRICK), BF),
            pltpu.VMEM((2, 2, 256, 256), BF),
            pltpu.VMEM((2, 512, 256), BF),
            pltpu.VMEM((256, 256), BF),
            pltpu.VMEM((2, 16, 256), BF),
            pltpu.VMEM((2, 128, 128), F),
            pltpu.VMEM((2 * 8 * 16, 128), F),
            pltpu.VMEM((2, 512, 256), BF),
            pltpu.VMEM((2, 512, 256), BF),
            pltpu.VMEM((64, 4, 128), F),
            pltpu.VMEM((64, 4, 128), F),
            pltpu.VMEM((2, 64, 128), jnp.int32),
            pltpu.VMEM((32, 128), BF),
            pltpu.VMEM((128, 128), BF),
            pltpu.VMEM((4, 128), BF),
            pltpu.VMEM((1, 128), F),
            pltpu.VMEM((1, 128), F),
            pltpu.VMEM((1, 4), F),
            pltpu.SemaphoreType.DMA((8,)),
            pltpu.SemaphoreType.DMA((7,)),
            pltpu.SemaphoreType.DMA,
            pltpu.SemaphoreType.DMA,
        ],
        compiler_params=pltpu.CompilerParams(
            collective_id=0, has_side_effects=True, vmem_limit_bytes=40 * 2**20
        ),
    )(
        *(
            pltpu.with_memory_space_constraint(operand, pltpu.HBM)
            for operand in (features, ray_spans.reshape(2, 64, 128))
        ),
        view_order,
        *(
            pltpu.with_memory_space_constraint(operand, pltpu.HBM)
            for operand in (
                w_first.T, w_second, w_last, b_first.reshape(1, 128), b_second.reshape(1, 128), b_last.reshape(1, 4)
            )
        ),
    )


def solution(mesh):
    return jax.shard_map(
        per_device,
        mesh=mesh,
        in_specs=(P(None, "depth", "tile"), P(None, "depth", "tile"), P("tile"), P(), P(), P(), P(), P(), P()),
        out_specs=P(None, ("tile", "depth")),
        check_vma=False,
    )
```

```python
import functools

import jax
import jax.numpy as jnp
from jax import lax
from jax.experimental import pallas as pl
from jax.experimental.pallas import tpu as pltpu
from jax.sharding import PartitionSpec as P

BF = jnp.bfloat16
F = jnp.float32
BRICK = 1024
CH = 32
MESH = pl.DeviceIdType.MESH
AWAY = (4, 3, 5, 2, 6, 1, 7, 0)
RING = tuple(min(a, 8 - a) for a in range(8))
PEERS = sorted(
    ((a, b) for a in range(8) for b in range(8) if a or b), key=lambda p: -(RING[p[0]] + RING[p[1]])
)
FAR = [(a, b) for a, b in PEERS if RING[a] + RING[b] >= 6]


def over(near, far):
    through = 1.0 - near[3]
    return [a + through * b for a, b in zip(near, far)]


def ordered(flip, first, second):
    near = [jnp.where(flip, b, a) for a, b in zip(first, second)]
    far = [jnp.where(flip, a, b) for a, b in zip(first, second)]
    return over(near, far)


def stack_samples(z_ref, spans, zrow, row, flip, b_last, spacing):
    entry = spans[0, pl.ds(row, 8), :]
    leave = spans[1, pl.ds(row, 8), :]
    remain, opacity = [], []
    for s in range(4):
        density = z_ref[pl.ds(zrow + 4 * s, 8, stride=16), :] + b_last[0]
        soft = jnp.maximum(density, 0.0) + jnp.log1p(jnp.exp(-jnp.abs(density)))
        kept = jnp.exp(soft * (-spacing))
        kept = jnp.where((entry <= s) & (leave > s), kept, 1.0)
        remain.append(kept)
        opacity.append(1.0 - kept)
    p01 = remain[0] * remain[1]
    p012 = p01 * remain[2]
    q32 = remain[3] * remain[2]
    q321 = q32 * remain[1]
    through = [
        jnp.where(flip, q321, 1.0),
        jnp.where(flip, q32, remain[0]),
        jnp.where(flip, remain[3], p01),
        jnp.where(flip, 1.0, p012),
    ]
    weight = [t * o for t, o in zip(through, opacity)]
    layers = []
    for ch in range(3):
        total = None
        for s in range(4):
            color = z_ref[pl.ds(zrow + 4 * s + 1 + ch, 8, stride=16), :] + b_last[1 + ch]
            term = weight[s] * (0.5 * jnp.tanh(0.5 * color) + 0.5)
            total = term if total is None else total + term
        layers.append(total)
    layers.append((weight[0] + weight[1]) + (weight[2] + weight[3]))
    return layers


def kernel(*refs, slabs):
    accs = []
    for m in range(2):
        accs += [pltpu.ACC(m)((CH, 256), F)] * 31 + [pltpu.ACC(m)((16, 256), F)] * 2
    pl.run_scoped(lambda *accs: body(*refs, accs=accs, slabs=slabs), *accs)


def body(
    x_hbm, spans_hbm, order, w1_hbm, w2_hbm, w3_hbm, b1_hbm, b2_hbm, bl_hbm, out,
    xbuf, xs, w1p, w2p, w3p, bias, z_ref, h1s, h2s, sent, taken,
    spans, w1t, w2, w3, b1, b2, bl, sem, small_sem, send_sem, hand_sem, recv_sem,
    *, accs, slabs,
):
    acc1 = [accs[m * 33 : m * 33 + 16] for m in range(2)]
    acc2 = [accs[m * 33 + 16 : m * 33 + 31] + accs[m * 33 + 16 : m * 33 + 17] for m in range(2)]
    acc3 = [accs[m * 33 + 31 : m * 33 + 33] for m in range(2)]
    bricks = 8
    me = lax.axis_index("depth")
    low = lax.rem(me, 8)
    high = lax.div(me, 8)
    spacing = 6.0 / (4 * slabs)

    barrier = pltpu.get_barrier_semaphore()

    def greet(dx, dz):
        peer = lax.rem(high + dx, 8) * 8 + lax.rem(low + dz, 8)
        pl.semaphore_signal(barrier, inc=1, device_id={"depth": peer}, device_id_type=MESH)

    @pl.when(low < 6)
    def _():
        for dx, dz in FAR:
            greet(dx, dz)

    for dx, dz in PEERS:
        if (dx, dz) not in FAR:
            greet(dx, dz)

    by_relay = jnp.where(
        (low == 2) | (low == 3), 8, jnp.where((low == 1) | (low == 4), 4, jnp.where((low == 0) | (low == 5), 1, 0))
    )

    def place(k):
        step = lax.div(k + 1, 2)
        away = jnp.where(lax.rem(k, 2) == 1, 4 - step, 4 + step)
        return lax.rem(high + lax.rem(away, 8), 8)

    def xcopy(k):
        start = pl.multiple_of(place(k) * BRICK, BRICK)
        return pltpu.make_async_copy(x_hbm.at[:, :, pl.ds(start, BRICK)], xbuf.at[k], sem.at[k])

    small = [
        pltpu.make_async_copy(src, dst, small_sem.at[i])
        for i, (src, dst) in enumerate(
            (
                (w1_hbm, w1t), (w2_hbm, w2), (w3_hbm, w3), (b1_hbm, b1), (b2_hbm, b2),
                (bl_hbm, bl), (spans_hbm, spans),
            )
        )
    ]
    for copy in small[:1]:
        copy.start()
    xcopy(0).start()
    for copy in small[1:]:
        copy.start()
    for k in range(1, bricks):
        xcopy(k).start()
    for copy in small:
        copy.wait()

    first = jnp.concatenate([w1t[...].astype(F), jnp.zeros((96, 128), F)], axis=0)
    first = jnp.transpose(first).astype(BF)
    first = jnp.concatenate([first, jnp.zeros((128, 128), BF)], axis=1)
    channel = lax.broadcasted_iota(jnp.int32, (256, 128), 0)
    column = lax.broadcasted_iota(jnp.int32, (256, 128), 1)
    for q in range(2):
        spread = jnp.concatenate(
            [(column == channel * 4 + (2 * q + k)).astype(F).astype(BF) for k in range(2)], axis=1
        )
        pltpu.matmul_push_rhs(spread, 0, q)
        for i in range(4):
            rows = first[i * CH : (i + 1) * CH]
            pltpu.matmul_acc_lhs(acc1[q][i], rows, load_staged_rhs=0 if i == 0 else None)
    for q in range(2):
        for i in range(4):
            wide = pltpu.matmul_pop(acc1[q][i]).astype(BF)
            for k in range(2):
                rows = pl.ds(q * 256 + k * 128 + i * CH, CH)
                for j in range(2):
                    w1p[j, rows, j * 128 : (j + 1) * 128] = wide[:, k * 128 : (k + 1) * 128]
                    w1p[j, rows, (1 - j) * 128 : (2 - j) * 128] = jnp.zeros((CH, 128), BF)
    for k in range(2):
        w2p[k * 128 : (k + 1) * 128, k * 128 : (k + 1) * 128] = w2[...]
        w2p[k * 128 : (k + 1) * 128, (1 - k) * 128 : (2 - k) * 128] = jnp.zeros((128, 128), BF)
    last = w3[...].astype(F)
    none = jnp.zeros((4, 128), F)
    for q in range(2):
        left = jnp.concatenate([last if s == 2 * q else none for s in range(4)], axis=0)
        right = jnp.concatenate([last if s == 2 * q + 1 else none for s in range(4)], axis=0)
        w3p[q] = jnp.concatenate([left, right], axis=1).astype(BF)
    bias[0] = jnp.transpose(jnp.broadcast_to(b1[...], (128, 128)))
    bias[1] = jnp.transpose(jnp.broadcast_to(b2[...], (128, 128)))
    flip = jnp.full((8, 128), order[0], jnp.int32) == 1
    b_last = [jnp.broadcast_to(bl[0:1, i : i + 1], (8, 128)) for i in range(4)]

    def prep(k):
        for m in range(2):
            for j in range(2):
                tile = xbuf[k, :, :, m * 512 + j * 256 : m * 512 + (j + 1) * 256]
                xs[lax.rem(k, 2), m, j * 128 : (j + 1) * 128, :] = tile.reshape(128, 256)

    def push(source, stage):
        for m in range(2):
            pltpu.matmul_push_rhs(source(m), stage, m)

    def mm1(j, i, stage):
        for m in range(2):
            rows = w1p[j, i * CH : (i + 1) * CH, :]
            pltpu.matmul_acc_lhs(acc1[m][i], rows, load_staged_rhs=stage if i == 0 else None)

    def mm2(i, stage):
        for m in range(2):
            rows = w2p[(i % 8) * CH : (i % 8 + 1) * CH, :]
            pltpu.matmul_acc_lhs(acc2[m][i], rows, load_staged_rhs=stage if i % 8 == 0 else None)

    def mm3(j, q, stage):
        for m in range(2):
            pltpu.matmul_acc_lhs(acc3[m][j], w3p[q], load_staged_rhs=stage)

    def settle(acc, layer, i, dst):
        r = (i * CH) % 128
        shift = bias[layer, r : r + CH, :]
        shift = jnp.concatenate([shift, shift], axis=1)
        for m in range(2):
            value = (pltpu.matmul_pop(acc[m][i]) + shift).astype(BF)
            dst[m, i * CH : (i + 1) * CH, :] = jnp.maximum(value, jnp.zeros((), BF))

    def pop3(j, par):
        for m in range(2):
            value = pltpu.matmul_pop(acc3[m][j])
            row = par * 128 + 32 * (2 * m + j)
            z_ref[pl.ds(row, 16), :] = value[:, :128]
            z_ref[pl.ds(row + 16, 16), :] = value[:, 128:]

    def slot(k, j, first=False, second=False, last=False, last_brick=False, middle=None, late=None):
        par = lax.rem(k, 2)
        s0, s1 = j % 2, 1 - j % 2
        push(lambda m: h1s[m, 0:256, :], s1)
        for i in range(16):
            if not last:
                mm1(1 - j, i, s0)
            if i >= 1 and not first:
                settle(acc2, 1, i, h2s)
            if i == 8 and not first:
                push(lambda m: h2s[m, 0:256, :], s0)
        if middle:
            middle()
        if not first and not second:
            pop3(j, 1 - par)
        for i in range(8):
            mm2(i, s1)
            if not last:
                settle(acc1, 0, i, h1s)
        push(lambda m: h1s[m, 256:512, :], s1)
        if not first:
            mm3(1 - j, 0, s0)
            push(lambda m: h2s[m, 256:512, :], s0)
        for i in range(8, 16):
            if i == 15:
                settle(acc2, 1, 0, h2s)
            mm2(i, s1)
            if not last:
                settle(acc1, 0, i, h1s)
        if late:
            late()
        if not last_brick:
            push(lambda m: xs[1 - par, m], s1)
        if not first:
            mm3(1 - j, 1, s0)

    def brick(k, first=False, last=False, late=None):
        if not last:
            xcopy(k + 1).wait()
        middle = None if last else lambda: prep(k + 1)
        slot(k, 0, first=first, last_brick=last, middle=middle)
        slot(k, 1, second=first, last=last, last_brick=last, late=late)

    def send(k, j):
        chunk = lax.rem(low + AWAY[j], 8)
        owner = place(k) * 8 + chunk
        way, target = 0, owner
        if RING[AWAY[j]] >= 2:
            far = (chunk >= 6) & (4 - lax.div(k + 1, 2) >= 6 - RING[AWAY[j]])
            way = jnp.where(far, 8 - chunk, 0)
            target = jnp.where(far, place(k) * 8, owner)
        return pltpu.make_async_remote_copy(
            src_ref=sent.at[k * 8 + chunk],
            dst_ref=taken.at[way, me],
            send_sem=send_sem,
            recv_sem=recv_sem.at[way],
            device_id={"depth": target},
            device_id_type=MESH,
        )

    def arrived(way, count):
        pltpu.make_async_remote_copy(
            src_ref=sent.at[pl.ds(0, count)],
            dst_ref=taken.at[0, pl.ds(0, count)],
            send_sem=send_sem,
            recv_sem=recv_sem.at[way],
            device_id={"depth": lax.rem(me + 1, slabs)},
            device_id_type=MESH,
        ).wait_recv()

    def hand_on(way):
        arrived(way, len(FAR))
        for dx, dz in FAR:
            source = lax.rem(high + 8 - dx, 8) * 8 + (16 - way - dz) % 8
            pltpu.make_async_remote_copy(
                src_ref=taken.at[way, source],
                dst_ref=taken.at[0, source],
                send_sem=hand_sem,
                recv_sem=recv_sem.at[3],
                device_id={"depth": high * 8 + 8 - way},
                device_id_type=MESH,
            ).start()

    def finish(k):
        row = pl.multiple_of(place(k) * 8, 8)
        layers = stack_samples(z_ref, spans, lax.rem(k, 2) * 128, row, flip, b_last, spacing)
        for ch in range(4):
            sent[pl.ds(k * 8, 8), ch, :] = layers[ch]

    def send_brick(k):
        for j in range(8):
            send(k, j).start()

    xcopy(0).wait()
    prep(0)
    push(lambda m: xs[0, m], 1)
    for i in range(16):
        mm1(0, i, 1)
    push(lambda m: xs[0, m], 0)
    for i in range(16):
        settle(acc1, 0, i, h1s)
    brick(0, first=True)

    def step(k, _):
        brick(k, late=lambda: finish(k - 1))

        @pl.when(k == 3)
        def _():
            pl.semaphore_wait(barrier, slabs - 1 - by_relay)
            send_brick(0)
            send_brick(1)

        @pl.when(k >= 3)
        def _():
            send_brick(k - 1)

        return 0

    lax.fori_loop(1, bricks - 1, step, 0)
    brick(bricks - 1, last=True, late=lambda: finish(bricks - 2))
    send_brick(bricks - 2)
    for i in range(1, 16):
        settle(acc2, 1, i, h2s)
    push(lambda m: h2s[m, 0:256, :], 0)
    push(lambda m: h2s[m, 256:512, :], 1)
    pop3(0, (bricks - 1) % 2)
    mm3(1, 0, 0)
    mm3(1, 1, 1)
    pop3(1, (bricks - 1) % 2)
    finish(bricks - 1)
    for j in range(7):
        send(bricks - 1, j).start()
    taken[0, me] = sent[(bricks - 1) * 8 + low]

    @pl.when(low == 0)
    def _():
        hand_on(2)
        hand_on(1)

    @pl.when(low < 6)
    def _():
        arrived(0, slabs - 1)

    @pl.when(low >= 6)
    def _():
        arrived(0, slabs - 1 - len(FAR))
        arrived(3, len(FAR))

    groups = [[taken[0, pl.ds(k, 8, stride=8), ch, :] for ch in range(4)] for k in range(8)]
    while len(groups) > 1:
        groups = [ordered(flip, a, b) for a, b in zip(groups[::2], groups[1::2])]
    total = groups[0]
    for shift in (7, 6, 4):
        total = ordered(flip, total, [pltpu.roll(c, shift, 0) for c in total])
    out[...] = jnp.concatenate([c[0:1] for c in total], axis=0)
    pltpu.make_async_remote_copy(
        src_ref=sent.at[pl.ds(0, slabs - 1)],
        dst_ref=taken.at[0, pl.ds(0, slabs - 1)],
        send_sem=send_sem,
        recv_sem=recv_sem.at[0],
        device_id={"depth": lax.rem(me + 1, slabs)},
        device_id_type=MESH,
    ).wait_send()

    @pl.when(low == 0)
    def _():
        pltpu.make_async_remote_copy(
            src_ref=sent.at[pl.ds(0, 2 * len(FAR))],
            dst_ref=taken.at[0, pl.ds(0, 2 * len(FAR))],
            send_sem=hand_sem,
            recv_sem=recv_sem.at[3],
            device_id={"depth": lax.rem(me + 1, slabs)},
            device_id_type=MESH,
        ).wait_send()


def per_device(features, ray_spans, view_order, w_first, b_first, w_second, b_second, w_last, b_last):
    slabs = lax.axis_size("depth")
    hbm = pl.BlockSpec(memory_space=pltpu.HBM)
    return pl.pallas_call(
        functools.partial(kernel, slabs=slabs),
        out_shape=jax.ShapeDtypeStruct((4, 128), F),
        in_specs=[hbm, hbm, pl.BlockSpec(memory_space=pltpu.SMEM)] + [hbm] * 6,
        out_specs=pl.BlockSpec(memory_space=pltpu.VMEM),
        scratch_shapes=[
            pltpu.VMEM((8, 32, 4, BRICK), BF),
            pltpu.VMEM((2, 2, 256, 256), BF),
            pltpu.VMEM((2, 512, 256), BF),
            pltpu.VMEM((256, 256), BF),
            pltpu.VMEM((2, 16, 256), BF),
            pltpu.VMEM((2, 128, 128), F),
            pltpu.VMEM((2 * 8 * 16, 128), F),
            pltpu.VMEM((2, 512, 256), BF),
            pltpu.VMEM((2, 512, 256), BF),
            pltpu.VMEM((64, 4, 128), F),
            pltpu.VMEM((3, 64, 4, 128), F),
            pltpu.VMEM((2, 64, 128), jnp.int32),
            pltpu.VMEM((32, 128), BF),
            pltpu.VMEM((128, 128), BF),
            pltpu.VMEM((4, 128), BF),
            pltpu.VMEM((1, 128), F),
            pltpu.VMEM((1, 128), F),
            pltpu.VMEM((1, 4), F),
            pltpu.SemaphoreType.DMA((8,)),
            pltpu.SemaphoreType.DMA((7,)),
            pltpu.SemaphoreType.DMA,
            pltpu.SemaphoreType.DMA,
            pltpu.SemaphoreType.DMA((4,)),
        ],
        compiler_params=pltpu.CompilerParams(
            collective_id=0, has_side_effects=True, vmem_limit_bytes=40 * 2**20
        ),
    )(
        *(
            pltpu.with_memory_space_constraint(operand, pltpu.HBM)
            for operand in (features, ray_spans.reshape(2, 64, 128))
        ),
        view_order,
        *(
            pltpu.with_memory_space_constraint(operand, pltpu.HBM)
            for operand in (
                w_first.T, w_second, w_last, b_first.reshape(1, 128), b_second.reshape(1, 128), b_last.reshape(1, 4)
            )
        ),
    )


def solution(mesh):
    return jax.shard_map(
        per_device,
        mesh=mesh,
        in_specs=(P(None, "depth", "tile"), P(None, "depth", "tile"), P("tile"), P(), P(), P(), P(), P(), P()),
        out_specs=P(None, ("tile", "depth")),
        check_vma=False,
    )
```

```python
import functools

import jax
import jax.numpy as jnp
from jax import lax
from jax.experimental import pallas as pl
from jax.experimental.pallas import tpu as pltpu
from jax.sharding import PartitionSpec as P

BF = jnp.bfloat16
F = jnp.float32
BRICK = 1024
CH = 32
MESH = pl.DeviceIdType.MESH
AWAY = (4, 3, 5, 2, 6, 1, 7, 0)
RING = tuple(min(a, 8 - a) for a in range(8))
PEERS = sorted(
    ((a, b) for a in range(8) for b in range(8) if a or b), key=lambda p: -(RING[p[0]] + RING[p[1]])
)
FAR = [(a, b) for a, b in PEERS if RING[a] + RING[b] >= 6]


def over(near, far):
    through = 1.0 - near[3]
    return [a + through * b for a, b in zip(near, far)]


def ordered(flip, first, second):
    near = [jnp.where(flip, b, a) for a, b in zip(first, second)]
    far = [jnp.where(flip, a, b) for a, b in zip(first, second)]
    return over(near, far)


def stack_samples(z_ref, spans, zrow, row, flip, b_last, spacing):
    entry = spans[0, pl.ds(row, 8), :]
    leave = spans[1, pl.ds(row, 8), :]
    remain, opacity = [], []
    for s in range(4):
        density = z_ref[pl.ds(zrow + 4 * s, 8, stride=16), :] + b_last[0]
        soft = jnp.maximum(density, 0.0) + jnp.log1p(jnp.exp(-jnp.abs(density)))
        kept = jnp.exp(soft * (-spacing))
        kept = jnp.where((entry <= s) & (leave > s), kept, 1.0)
        remain.append(kept)
        opacity.append(1.0 - kept)
    p01 = remain[0] * remain[1]
    p012 = p01 * remain[2]
    q32 = remain[3] * remain[2]
    q321 = q32 * remain[1]
    through = [
        jnp.where(flip, q321, 1.0),
        jnp.where(flip, q32, remain[0]),
        jnp.where(flip, remain[3], p01),
        jnp.where(flip, 1.0, p012),
    ]
    weight = [t * o for t, o in zip(through, opacity)]
    layers = []
    for ch in range(3):
        total = None
        for s in range(4):
            color = z_ref[pl.ds(zrow + 4 * s + 1 + ch, 8, stride=16), :] + b_last[1 + ch]
            term = weight[s] * (0.5 * jnp.tanh(0.5 * color) + 0.5)
            total = term if total is None else total + term
        layers.append(total)
    layers.append((weight[0] + weight[1]) + (weight[2] + weight[3]))
    return layers


def kernel(*refs, slabs):
    accs = []
    for m in range(2):
        accs += [pltpu.ACC(m)((CH, 256), F)] * 31 + [pltpu.ACC(m)((16, 256), F)] * 2
    pl.run_scoped(lambda *accs: body(*refs, accs=accs, slabs=slabs), *accs)


def body(
    x_hbm, spans_hbm, order, w1_hbm, w2_hbm, w3_hbm, b1_hbm, b2_hbm, bl_hbm, out,
    xbuf, xs, w1p, w2p, w3p, bias, z_ref, h1s, h2s, sent, taken,
    spans, w1t, w2, w3, b1, b2, bl, sem, small_sem, send_sem, hand_sem, recv_sem,
    *, accs, slabs,
):
    acc1 = [accs[m * 33 : m * 33 + 16] for m in range(2)]
    acc2 = [accs[m * 33 + 16 : m * 33 + 31] + accs[m * 33 + 16 : m * 33 + 17] for m in range(2)]
    acc3 = [accs[m * 33 + 31 : m * 33 + 33] for m in range(2)]
    bricks = 8
    me = lax.axis_index("depth")
    low = lax.rem(me, 8)
    high = lax.div(me, 8)
    mirrored = lax.rem(lax.axis_index("tile"), 2) == 1
    spacing = 6.0 / (4 * slabs)

    barrier = pltpu.get_barrier_semaphore()

    def greet(dx, dz):
        peer = lax.rem(high + dx, 8) * 8 + lax.rem(low + dz, 8)
        pl.semaphore_signal(barrier, inc=1, device_id={"depth": peer}, device_id_type=MESH)

    @pl.when(low < 6)
    def _():
        for dx, dz in FAR:
            greet(dx, dz)

    for dx, dz in PEERS:
        if (dx, dz) not in FAR:
            greet(dx, dz)

    by_relay = jnp.where(
        (low == 2) | (low == 3), 8, jnp.where((low == 1) | (low == 4), 4, jnp.where((low == 0) | (low == 5), 1, 0))
    )

    def place(k):
        step = lax.div(k + 1, 2)
        away = jnp.where(lax.rem(k, 2) == 1, 4 - step, 4 + step)
        return lax.rem(high + jnp.where(mirrored, 8 - away, away), 8)

    def xcopy(k):
        start = pl.multiple_of(place(k) * BRICK, BRICK)
        return pltpu.make_async_copy(x_hbm.at[:, :, pl.ds(start, BRICK)], xbuf.at[k], sem.at[k])

    small = [
        pltpu.make_async_copy(src, dst, small_sem.at[i])
        for i, (src, dst) in enumerate(
            (
                (w1_hbm, w1t), (w2_hbm, w2), (w3_hbm, w3), (b1_hbm, b1), (b2_hbm, b2),
                (bl_hbm, bl), (spans_hbm, spans),
            )
        )
    ]
    for copy in small[:1]:
        copy.start()
    xcopy(0).start()
    for copy in small[1:]:
        copy.start()
    for k in range(1, bricks):
        xcopy(k).start()
    for copy in small:
        copy.wait()

    first = jnp.concatenate([w1t[...].astype(F), jnp.zeros((96, 128), F)], axis=0)
    first = jnp.transpose(first).astype(BF)
    first = jnp.concatenate([first, jnp.zeros((128, 128), BF)], axis=1)
    channel = lax.broadcasted_iota(jnp.int32, (256, 128), 0)
    column = lax.broadcasted_iota(jnp.int32, (256, 128), 1)
    for q in range(2):
        spread = jnp.concatenate(
            [(column == channel * 4 + (2 * q + k)).astype(F).astype(BF) for k in range(2)], axis=1
        )
        pltpu.matmul_push_rhs(spread, 0, q)
        for i in range(4):
            rows = first[i * CH : (i + 1) * CH]
            pltpu.matmul_acc_lhs(acc1[q][i], rows, load_staged_rhs=0 if i == 0 else None)
    for q in range(2):
        for i in range(4):
            wide = pltpu.matmul_pop(acc1[q][i]).astype(BF)
            for k in range(2):
                rows = pl.ds(q * 256 + k * 128 + i * CH, CH)
                for j in range(2):
                    w1p[j, rows, j * 128 : (j + 1) * 128] = wide[:, k * 128 : (k + 1) * 128]
                    w1p[j, rows, (1 - j) * 128 : (2 - j) * 128] = jnp.zeros((CH, 128), BF)
    for k in range(2):
        w2p[k * 128 : (k + 1) * 128, k * 128 : (k + 1) * 128] = w2[...]
        w2p[k * 128 : (k + 1) * 128, (1 - k) * 128 : (2 - k) * 128] = jnp.zeros((128, 128), BF)
    last = w3[...].astype(F)
    none = jnp.zeros((4, 128), F)
    for q in range(2):
        left = jnp.concatenate([last if s == 2 * q else none for s in range(4)], axis=0)
        right = jnp.concatenate([last if s == 2 * q + 1 else none for s in range(4)], axis=0)
        w3p[q] = jnp.concatenate([left, right], axis=1).astype(BF)
    bias[0] = jnp.transpose(jnp.broadcast_to(b1[...], (128, 128)))
    bias[1] = jnp.transpose(jnp.broadcast_to(b2[...], (128, 128)))
    flip = jnp.full((8, 128), order[0], jnp.int32) == 1
    b_last = [jnp.broadcast_to(bl[0:1, i : i + 1], (8, 128)) for i in range(4)]

    def prep(k):
        for m in range(2):
            for j in range(2):
                tile = xbuf[k, :, :, m * 512 + j * 256 : m * 512 + (j + 1) * 256]
                xs[lax.rem(k, 2), m, j * 128 : (j + 1) * 128, :] = tile.reshape(128, 256)

    def push(source, stage):
        for m in range(2):
            pltpu.matmul_push_rhs(source(m), stage, m)

    def mm1(j, i, stage):
        for m in range(2):
            rows = w1p[j, i * CH : (i + 1) * CH, :]
            pltpu.matmul_acc_lhs(acc1[m][i], rows, load_staged_rhs=stage if i == 0 else None)

    def mm2(i, stage):
        for m in range(2):
            rows = w2p[(i % 8) * CH : (i % 8 + 1) * CH, :]
            pltpu.matmul_acc_lhs(acc2[m][i], rows, load_staged_rhs=stage if i % 8 == 0 else None)

    def mm3(j, q, stage):
        for m in range(2):
            pltpu.matmul_acc_lhs(acc3[m][j], w3p[q], load_staged_rhs=stage)

    def settle(acc, layer, i, dst):
        r = (i * CH) % 128
        shift = bias[layer, r : r + CH, :]
        shift = jnp.concatenate([shift, shift], axis=1)
        for m in range(2):
            value = (pltpu.matmul_pop(acc[m][i]) + shift).astype(BF)
            dst[m, i * CH : (i + 1) * CH, :] = jnp.maximum(value, jnp.zeros((), BF))

    def pop3(j, par):
        for m in range(2):
            value = pltpu.matmul_pop(acc3[m][j])
            row = par * 128 + 32 * (2 * m + j)
            z_ref[pl.ds(row, 16), :] = value[:, :128]
            z_ref[pl.ds(row + 16, 16), :] = value[:, 128:]

    def slot(k, j, first=False, second=False, last=False, last_brick=False, middle=None, late=None):
        par = lax.rem(k, 2)
        s0, s1 = j % 2, 1 - j % 2
        push(lambda m: h1s[m, 0:256, :], s1)
        for i in range(16):
            if not last:
                mm1(1 - j, i, s0)
            if i >= 1 and not first:
                settle(acc2, 1, i, h2s)
            if i == 8 and not first:
                push(lambda m: h2s[m, 0:256, :], s0)
        if middle:
            middle()
        if not first and not second:
            pop3(j, 1 - par)
        for i in range(8):
            mm2(i, s1)
            if not last:
                settle(acc1, 0, i, h1s)
        push(lambda m: h1s[m, 256:512, :], s1)
        if not first:
            mm3(1 - j, 0, s0)
            push(lambda m: h2s[m, 256:512, :], s0)
        for i in range(8, 16):
            if i == 15:
                settle(acc2, 1, 0, h2s)
            mm2(i, s1)
            if not last:
                settle(acc1, 0, i, h1s)
        if late:
            late()
        if not last_brick:
            push(lambda m: xs[1 - par, m], s1)
        if not first:
            mm3(1 - j, 1, s0)

    def brick(k, first=False, last=False, late=None):
        if not last:
            xcopy(k + 1).wait()
        middle = None if last else lambda: prep(k + 1)
        slot(k, 0, first=first, last_brick=last, middle=middle)
        slot(k, 1, second=first, last=last, last_brick=last, late=late)

    def send(k, j):
        chunk = lax.rem(low + jnp.where(mirrored, 8 - AWAY[j], AWAY[j]), 8)
        owner = place(k) * 8 + chunk
        way, target = 0, owner
        if RING[AWAY[j]] >= 2:
            far = (chunk >= 6) & (4 - lax.div(k + 1, 2) >= 6 - RING[AWAY[j]])
            way = jnp.where(far, 8 - chunk, 0)
            target = jnp.where(far, place(k) * 8, owner)
        return pltpu.make_async_remote_copy(
            src_ref=sent.at[k * 8 + chunk],
            dst_ref=taken.at[way, me],
            send_sem=send_sem,
            recv_sem=recv_sem.at[way],
            device_id={"depth": target},
            device_id_type=MESH,
        )

    def arrived(way, count):
        pltpu.make_async_remote_copy(
            src_ref=sent.at[pl.ds(0, count)],
            dst_ref=taken.at[0, pl.ds(0, count)],
            send_sem=send_sem,
            recv_sem=recv_sem.at[way],
            device_id={"depth": lax.rem(me + 1, slabs)},
            device_id_type=MESH,
        ).wait_recv()

    def hand_on(way):
        arrived(way, len(FAR))
        for dx, dz in FAR:
            source = lax.rem(high + 8 - dx, 8) * 8 + (16 - way - dz) % 8
            pltpu.make_async_remote_copy(
                src_ref=taken.at[way, source],
                dst_ref=taken.at[0, source],
                send_sem=hand_sem,
                recv_sem=recv_sem.at[3],
                device_id={"depth": high * 8 + 8 - way},
                device_id_type=MESH,
            ).start()

    def finish(k):
        row = pl.multiple_of(place(k) * 8, 8)
        layers = stack_samples(z_ref, spans, lax.rem(k, 2) * 128, row, flip, b_last, spacing)
        for ch in range(4):
            sent[pl.ds(k * 8, 8), ch, :] = layers[ch]

    def send_brick(k):
        for j in range(8):
            send(k, j).start()

    xcopy(0).wait()
    prep(0)
    push(lambda m: xs[0, m], 1)
    for i in range(16):
        mm1(0, i, 1)
    push(lambda m: xs[0, m], 0)
    for i in range(16):
        settle(acc1, 0, i, h1s)
    brick(0, first=True)

    def step(k, _):
        brick(k, late=lambda: finish(k - 1))

        @pl.when(k == 3)
        def _():
            pl.semaphore_wait(barrier, slabs - 1 - by_relay)
            send_brick(0)
            send_brick(1)

        @pl.when(k >= 3)
        def _():
            send_brick(k - 1)

        return 0

    lax.fori_loop(1, bricks - 1, step, 0)
    brick(bricks - 1, last=True, late=lambda: finish(bricks - 2))
    send_brick(bricks - 2)
    for i in range(1, 16):
        settle(acc2, 1, i, h2s)
    push(lambda m: h2s[m, 0:256, :], 0)
    push(lambda m: h2s[m, 256:512, :], 1)
    pop3(0, (bricks - 1) % 2)
    mm3(1, 0, 0)
    mm3(1, 1, 1)
    pop3(1, (bricks - 1) % 2)
    finish(bricks - 1)
    for j in range(7):
        send(bricks - 1, j).start()
    taken[0, me] = sent[(bricks - 1) * 8 + low]

    @pl.when(low == 0)
    def _():
        hand_on(2)
        hand_on(1)

    @pl.when(low < 6)
    def _():
        arrived(0, slabs - 1)

    @pl.when(low >= 6)
    def _():
        arrived(0, slabs - 1 - len(FAR))
        arrived(3, len(FAR))

    groups = [[taken[0, pl.ds(k, 8, stride=8), ch, :] for ch in range(4)] for k in range(8)]
    while len(groups) > 1:
        groups = [ordered(flip, a, b) for a, b in zip(groups[::2], groups[1::2])]
    total = groups[0]
    for shift in (7, 6, 4):
        total = ordered(flip, total, [pltpu.roll(c, shift, 0) for c in total])
    out[...] = jnp.concatenate([c[0:1] for c in total], axis=0)
    pltpu.make_async_remote_copy(
        src_ref=sent.at[pl.ds(0, slabs - 1)],
        dst_ref=taken.at[0, pl.ds(0, slabs - 1)],
        send_sem=send_sem,
        recv_sem=recv_sem.at[0],
        device_id={"depth": lax.rem(me + 1, slabs)},
        device_id_type=MESH,
    ).wait_send()

    @pl.when(low == 0)
    def _():
        pltpu.make_async_remote_copy(
            src_ref=sent.at[pl.ds(0, 2 * len(FAR))],
            dst_ref=taken.at[0, pl.ds(0, 2 * len(FAR))],
            send_sem=hand_sem,
            recv_sem=recv_sem.at[3],
            device_id={"depth": lax.rem(me + 1, slabs)},
            device_id_type=MESH,
        ).wait_send()


def per_device(features, ray_spans, view_order, w_first, b_first, w_second, b_second, w_last, b_last):
    slabs = lax.axis_size("depth")
    hbm = pl.BlockSpec(memory_space=pltpu.HBM)
    return pl.pallas_call(
        functools.partial(kernel, slabs=slabs),
        out_shape=jax.ShapeDtypeStruct((4, 128), F),
        in_specs=[hbm, hbm, pl.BlockSpec(memory_space=pltpu.SMEM)] + [hbm] * 6,
        out_specs=pl.BlockSpec(memory_space=pltpu.VMEM),
        scratch_shapes=[
            pltpu.VMEM((8, 32, 4, BRICK), BF),
            pltpu.VMEM((2, 2, 256, 256), BF),
            pltpu.VMEM((2, 512, 256), BF),
            pltpu.VMEM((256, 256), BF),
            pltpu.VMEM((2, 16, 256), BF),
            pltpu.VMEM((2, 128, 128), F),
            pltpu.VMEM((2 * 8 * 16, 128), F),
            pltpu.VMEM((2, 512, 256), BF),
            pltpu.VMEM((2, 512, 256), BF),
            pltpu.VMEM((64, 4, 128), F),
            pltpu.VMEM((3, 64, 4, 128), F),
            pltpu.VMEM((2, 64, 128), jnp.int32),
            pltpu.VMEM((32, 128), BF),
            pltpu.VMEM((128, 128), BF),
            pltpu.VMEM((4, 128), BF),
            pltpu.VMEM((1, 128), F),
            pltpu.VMEM((1, 128), F),
            pltpu.VMEM((1, 4), F),
            pltpu.SemaphoreType.DMA((8,)),
            pltpu.SemaphoreType.DMA((7,)),
            pltpu.SemaphoreType.DMA,
            pltpu.SemaphoreType.DMA,
            pltpu.SemaphoreType.DMA((4,)),
        ],
        compiler_params=pltpu.CompilerParams(
            collective_id=0, has_side_effects=True, vmem_limit_bytes=40 * 2**20
        ),
    )(
        *(
            pltpu.with_memory_space_constraint(operand, pltpu.HBM)
            for operand in (features, ray_spans.reshape(2, 64, 128))
        ),
        view_order,
        *(
            pltpu.with_memory_space_constraint(operand, pltpu.HBM)
            for operand in (
                w_first.T, w_second, w_last, b_first.reshape(1, 128), b_second.reshape(1, 128), b_last.reshape(1, 4)
            )
        ),
    )


def solution(mesh):
    return jax.shard_map(
        per_device,
        mesh=mesh,
        in_specs=(P(None, "depth", "tile"), P(None, "depth", "tile"), P("tile"), P(), P(), P(), P(), P(), P()),
        out_specs=P(None, ("tile", "depth")),
        check_vma=False,
    )
```

```python
import functools

import jax
import jax.numpy as jnp
from jax import lax
from jax.experimental import pallas as pl
from jax.experimental.pallas import tpu as pltpu
from jax.sharding import PartitionSpec as P

BF = jnp.bfloat16
F = jnp.float32
BRICK = 1024
CH = 32
MESH = pl.DeviceIdType.MESH
AWAY = (4, 3, 5, 2, 6, 1, 7, 0)
RING = tuple(min(a, 8 - a) for a in range(8))
PEERS = sorted(
    ((a, b) for a in range(8) for b in range(8) if a or b), key=lambda p: -(RING[p[0]] + RING[p[1]])
)
FAR = [(a, b) for a, b in PEERS if RING[a] + RING[b] >= 6]


def over(near, far):
    through = 1.0 - near[3]
    return [a + through * b for a, b in zip(near, far)]


def ordered(flip, first, second):
    near = [jnp.where(flip, b, a) for a, b in zip(first, second)]
    far = [jnp.where(flip, a, b) for a, b in zip(first, second)]
    return over(near, far)


def stack_samples(z_ref, spans, zrow, row, flip, b_last, spacing):
    entry = spans[0, pl.ds(row, 8), :]
    leave = spans[1, pl.ds(row, 8), :]
    remain, opacity = [], []
    for s in range(4):
        density = z_ref[pl.ds(zrow + 4 * s, 8, stride=16), :] + b_last[0]
        soft = jnp.maximum(density, 0.0) + jnp.log1p(jnp.exp(-jnp.abs(density)))
        kept = jnp.exp(soft * (-spacing))
        kept = jnp.where((entry <= s) & (leave > s), kept, 1.0)
        remain.append(kept)
        opacity.append(1.0 - kept)
    p01 = remain[0] * remain[1]
    p012 = p01 * remain[2]
    q32 = remain[3] * remain[2]
    q321 = q32 * remain[1]
    through = [
        jnp.where(flip, q321, 1.0),
        jnp.where(flip, q32, remain[0]),
        jnp.where(flip, remain[3], p01),
        jnp.where(flip, 1.0, p012),
    ]
    weight = [t * o for t, o in zip(through, opacity)]
    layers = []
    for ch in range(3):
        total = None
        for s in range(4):
            color = z_ref[pl.ds(zrow + 4 * s + 1 + ch, 8, stride=16), :] + b_last[1 + ch]
            term = weight[s] * (0.5 * jnp.tanh(0.5 * color) + 0.5)
            total = term if total is None else total + term
        layers.append(total)
    layers.append((weight[0] + weight[1]) + (weight[2] + weight[3]))
    return layers


def kernel(*refs, slabs):
    accs = []
    for m in range(2):
        accs += [pltpu.ACC(m)((CH, 256), F)] * 31 + [pltpu.ACC(m)((16, 256), F)] * 2
    pl.run_scoped(lambda *accs: body(*refs, accs=accs, slabs=slabs), *accs)


def body(
    x_hbm, spans_hbm, order, w1_hbm, w2_hbm, w3_hbm, b1_hbm, b2_hbm, bl_hbm, out,
    xbuf, xs, w1p, w2p, w3p, bias, z_ref, h1s, h2s, sent, taken,
    spans, w1t, w2, w3, b1, b2, bl, sem, small_sem, send_sem, hand_sem, recv_sem,
    *, accs, slabs,
):
    acc1 = [accs[m * 33 : m * 33 + 16] for m in range(2)]
    acc2 = [accs[m * 33 + 16 : m * 33 + 31] + accs[m * 33 + 16 : m * 33 + 17] for m in range(2)]
    acc3 = [accs[m * 33 + 31 : m * 33 + 33] for m in range(2)]
    bricks = 8
    me = lax.axis_index("depth")
    low = lax.rem(me, 8)
    high = lax.div(me, 8)
    mirrored = lax.rem(lax.axis_index("tile"), 2) == 1
    spacing = 6.0 / (4 * slabs)

    def place(k):
        step = lax.div(k + 1, 2)
        away = jnp.where(lax.rem(k, 2) == 1, 4 - step, 4 + step)
        return lax.rem(high + jnp.where(mirrored, 8 - away, away), 8)

    def xcopy(k):
        start = pl.multiple_of(place(k) * BRICK, BRICK)
        return pltpu.make_async_copy(x_hbm.at[:, :, pl.ds(start, BRICK)], xbuf.at[k], sem.at[k])

    small = [
        pltpu.make_async_copy(src, dst, small_sem.at[i])
        for i, (src, dst) in enumerate(
            (
                (w1_hbm, w1t), (w2_hbm, w2), (w3_hbm, w3), (b1_hbm, b1), (b2_hbm, b2),
                (bl_hbm, bl), (spans_hbm, spans),
            )
        )
    ]
    for copy in small[:1]:
        copy.start()
    xcopy(0).start()
    for copy in small[1:]:
        copy.start()
    for k in range(1, bricks):
        xcopy(k).start()

    barrier = pltpu.get_barrier_semaphore()

    def greet(dx, dz):
        peer = lax.rem(high + dx, 8) * 8 + lax.rem(low + dz, 8)
        pl.semaphore_signal(barrier, inc=1, device_id={"depth": peer}, device_id_type=MESH)

    @pl.when(low < 6)
    def _():
        for dx, dz in FAR:
            greet(dx, dz)

    for dx, dz in PEERS:
        if (dx, dz) not in FAR:
            greet(dx, dz)

    by_relay = jnp.where(
        (low == 2) | (low == 3), 8, jnp.where((low == 1) | (low == 4), 4, jnp.where((low == 0) | (low == 5), 1, 0))
    )

    for copy in small:
        copy.wait()

    first = jnp.concatenate([w1t[...].astype(F), jnp.zeros((96, 128), F)], axis=0)
    first = jnp.transpose(first).astype(BF)
    first = jnp.concatenate([first, jnp.zeros((128, 128), BF)], axis=1)
    channel = lax.broadcasted_iota(jnp.int32, (256, 128), 0)
    column = lax.broadcasted_iota(jnp.int32, (256, 128), 1)
    for q in range(2):
        spread = jnp.concatenate(
            [(column == channel * 4 + (2 * q + k)).astype(F).astype(BF) for k in range(2)], axis=1
        )
        pltpu.matmul_push_rhs(spread, 0, q)
        for i in range(4):
            rows = first[i * CH : (i + 1) * CH]
            pltpu.matmul_acc_lhs(acc1[q][i], rows, load_staged_rhs=0 if i == 0 else None)
    for q in range(2):
        for i in range(4):
            wide = pltpu.matmul_pop(acc1[q][i]).astype(BF)
            for k in range(2):
                rows = pl.ds(q * 256 + k * 128 + i * CH, CH)
                for j in range(2):
                    w1p[j, rows, j * 128 : (j + 1) * 128] = wide[:, k * 128 : (k + 1) * 128]
                    w1p[j, rows, (1 - j) * 128 : (2 - j) * 128] = jnp.zeros((CH, 128), BF)
    for k in range(2):
        w2p[k * 128 : (k + 1) * 128, k * 128 : (k + 1) * 128] = w2[...]
        w2p[k * 128 : (k + 1) * 128, (1 - k) * 128 : (2 - k) * 128] = jnp.zeros((128, 128), BF)
    last = w3[...].astype(F)
    none = jnp.zeros((4, 128), F)
    for q in range(2):
        left = jnp.concatenate([last if s == 2 * q else none for s in range(4)], axis=0)
        right = jnp.concatenate([last if s == 2 * q + 1 else none for s in range(4)], axis=0)
        w3p[q] = jnp.concatenate([left, right], axis=1).astype(BF)
    bias[0] = jnp.transpose(jnp.broadcast_to(b1[...], (128, 128)))
    bias[1] = jnp.transpose(jnp.broadcast_to(b2[...], (128, 128)))
    flip = jnp.full((8, 128), order[0], jnp.int32) == 1
    b_last = [jnp.broadcast_to(bl[0:1, i : i + 1], (8, 128)) for i in range(4)]

    def prep(k):
        for m in range(2):
            for j in range(2):
                tile = xbuf[k, :, :, m * 512 + j * 256 : m * 512 + (j + 1) * 256]
                xs[lax.rem(k, 2), m, j * 128 : (j + 1) * 128, :] = tile.reshape(128, 256)

    def push(source, stage):
        for m in range(2):
            pltpu.matmul_push_rhs(source(m), stage, m)

    def mm1(j, i, stage):
        for m in range(2):
            rows = w1p[j, i * CH : (i + 1) * CH, :]
            pltpu.matmul_acc_lhs(acc1[m][i], rows, load_staged_rhs=stage if i == 0 else None)

    def mm2(i, stage):
        for m in range(2):
            rows = w2p[(i % 8) * CH : (i % 8 + 1) * CH, :]
            pltpu.matmul_acc_lhs(acc2[m][i], rows, load_staged_rhs=stage if i % 8 == 0 else None)

    def mm3(j, q, stage):
        for m in range(2):
            pltpu.matmul_acc_lhs(acc3[m][j], w3p[q], load_staged_rhs=stage)

    def settle(acc, layer, i, dst):
        r = (i * CH) % 128
        shift = bias[layer, r : r + CH, :]
        shift = jnp.concatenate([shift, shift], axis=1)
        for m in range(2):
            value = (pltpu.matmul_pop(acc[m][i]) + shift).astype(BF)
            dst[m, i * CH : (i + 1) * CH, :] = jnp.maximum(value, jnp.zeros((), BF))

    def pop3(j, par):
        for m in range(2):
            value = pltpu.matmul_pop(acc3[m][j])
            row = par * 128 + 32 * (2 * m + j)
            z_ref[pl.ds(row, 16), :] = value[:, :128]
            z_ref[pl.ds(row + 16, 16), :] = value[:, 128:]

    def slot(k, j, first=False, second=False, last=False, last_brick=False, middle=None, late=None):
        par = lax.rem(k, 2)
        s0, s1 = j % 2, 1 - j % 2
        push(lambda m: h1s[m, 0:256, :], s1)
        for i in range(16):
            if not last:
                mm1(1 - j, i, s0)
            if i >= 1 and not first:
                settle(acc2, 1, i, h2s)
            if i == 8 and not first:
                push(lambda m: h2s[m, 0:256, :], s0)
        if middle:
            middle()
        if not first and not second:
            pop3(j, 1 - par)
        for i in range(8):
            mm2(i, s1)
            if not last:
                settle(acc1, 0, i, h1s)
        push(lambda m: h1s[m, 256:512, :], s1)
        if not first:
            mm3(1 - j, 0, s0)
            push(lambda m: h2s[m, 256:512, :], s0)
        for i in range(8, 16):
            if i == 15:
                settle(acc2, 1, 0, h2s)
            mm2(i, s1)
            if not last:
                settle(acc1, 0, i, h1s)
        if late:
            late()
        if not last_brick:
            push(lambda m: xs[1 - par, m], s1)
        if not first:
            mm3(1 - j, 1, s0)

    def brick(k, first=False, last=False, late=None):
        if not last:
            xcopy(k + 1).wait()
        middle = None if last else lambda: prep(k + 1)
        slot(k, 0, first=first, last_brick=last, middle=middle)
        slot(k, 1, second=first, last=last, last_brick=last, late=late)

    def send(k, j):
        chunk = lax.rem(low + jnp.where(mirrored, 8 - AWAY[j], AWAY[j]), 8)
        owner = place(k) * 8 + chunk
        way, target = 0, owner
        if RING[AWAY[j]] >= 2:
            far = (chunk >= 6) & (4 - lax.div(k + 1, 2) >= 6 - RING[AWAY[j]])
            way = jnp.where(far, 8 - chunk, 0)
            target = jnp.where(far, place(k) * 8, owner)
        return pltpu.make_async_remote_copy(
            src_ref=sent.at[k * 8 + chunk],
            dst_ref=taken.at[way, me],
            send_sem=send_sem,
            recv_sem=recv_sem.at[way],
            device_id={"depth": target},
            device_id_type=MESH,
        )

    def arrived(way, count):
        pltpu.make_async_remote_copy(
            src_ref=sent.at[pl.ds(0, count)],
            dst_ref=taken.at[0, pl.ds(0, count)],
            send_sem=send_sem,
            recv_sem=recv_sem.at[way],
            device_id={"depth": lax.rem(me + 1, slabs)},
            device_id_type=MESH,
        ).wait_recv()

    def hand_on(way):
        arrived(way, len(FAR))
        for dx, dz in FAR:
            source = lax.rem(high + 8 - dx, 8) * 8 + (16 - way - dz) % 8
            pltpu.make_async_remote_copy(
                src_ref=taken.at[way, source],
                dst_ref=taken.at[0, source],
                send_sem=hand_sem,
                recv_sem=recv_sem.at[3],
                device_id={"depth": high * 8 + 8 - way},
                device_id_type=MESH,
            ).start()

    def finish(k):
        row = pl.multiple_of(place(k) * 8, 8)
        layers = stack_samples(z_ref, spans, lax.rem(k, 2) * 128, row, flip, b_last, spacing)
        for ch in range(4):
            sent[pl.ds(k * 8, 8), ch, :] = layers[ch]

    def send_brick(k):
        for j in range(8):
            send(k, j).start()

    xcopy(0).wait()
    prep(0)
    push(lambda m: xs[0, m], 1)
    for i in range(16):
        mm1(0, i, 1)
    push(lambda m: xs[0, m], 0)
    for i in range(16):
        settle(acc1, 0, i, h1s)
    brick(0, first=True)

    def step(k, _):
        brick(k, late=lambda: finish(k - 1))

        @pl.when(k == 3)
        def _():
            pl.semaphore_wait(barrier, slabs - 1 - by_relay)
            send_brick(0)
            send_brick(1)

        @pl.when(k >= 3)
        def _():
            send_brick(k - 1)

        return 0

    lax.fori_loop(1, bricks - 1, step, 0)
    brick(bricks - 1, last=True, late=lambda: finish(bricks - 2))
    send_brick(bricks - 2)
    for i in range(1, 16):
        settle(acc2, 1, i, h2s)
    push(lambda m: h2s[m, 0:256, :], 0)
    push(lambda m: h2s[m, 256:512, :], 1)
    pop3(0, (bricks - 1) % 2)
    mm3(1, 0, 0)
    mm3(1, 1, 1)
    pop3(1, (bricks - 1) % 2)
    finish(bricks - 1)
    for j in range(7):
        send(bricks - 1, j).start()
    taken[0, me] = sent[(bricks - 1) * 8 + low]

    @pl.when(low == 0)
    def _():
        hand_on(2)
        hand_on(1)

    @pl.when(low < 6)
    def _():
        arrived(0, slabs - 1)

    @pl.when(low >= 6)
    def _():
        arrived(0, slabs - 1 - len(FAR))
        arrived(3, len(FAR))

    groups = [[taken[0, pl.ds(k, 8, stride=8), ch, :] for ch in range(4)] for k in range(8)]
    while len(groups) > 1:
        groups = [ordered(flip, a, b) for a, b in zip(groups[::2], groups[1::2])]
    total = groups[0]
    for shift in (7, 6, 4):
        total = ordered(flip, total, [pltpu.roll(c, shift, 0) for c in total])
    out[...] = jnp.concatenate([c[0:1] for c in total], axis=0)
    pltpu.make_async_remote_copy(
        src_ref=sent.at[pl.ds(0, slabs - 1)],
        dst_ref=taken.at[0, pl.ds(0, slabs - 1)],
        send_sem=send_sem,
        recv_sem=recv_sem.at[0],
        device_id={"depth": lax.rem(me + 1, slabs)},
        device_id_type=MESH,
    ).wait_send()

    @pl.when(low == 0)
    def _():
        pltpu.make_async_remote_copy(
            src_ref=sent.at[pl.ds(0, 2 * len(FAR))],
            dst_ref=taken.at[0, pl.ds(0, 2 * len(FAR))],
            send_sem=hand_sem,
            recv_sem=recv_sem.at[3],
            device_id={"depth": lax.rem(me + 1, slabs)},
            device_id_type=MESH,
        ).wait_send()


def per_device(features, ray_spans, view_order, w_first, b_first, w_second, b_second, w_last, b_last):
    slabs = lax.axis_size("depth")
    hbm = pl.BlockSpec(memory_space=pltpu.HBM)
    return pl.pallas_call(
        functools.partial(kernel, slabs=slabs),
        out_shape=jax.ShapeDtypeStruct((4, 128), F),
        in_specs=[hbm, hbm, pl.BlockSpec(memory_space=pltpu.SMEM)] + [hbm] * 6,
        out_specs=pl.BlockSpec(memory_space=pltpu.VMEM),
        scratch_shapes=[
            pltpu.VMEM((8, 32, 4, BRICK), BF),
            pltpu.VMEM((2, 2, 256, 256), BF),
            pltpu.VMEM((2, 512, 256), BF),
            pltpu.VMEM((256, 256), BF),
            pltpu.VMEM((2, 16, 256), BF),
            pltpu.VMEM((2, 128, 128), F),
            pltpu.VMEM((2 * 8 * 16, 128), F),
            pltpu.VMEM((2, 512, 256), BF),
            pltpu.VMEM((2, 512, 256), BF),
            pltpu.VMEM((64, 4, 128), F),
            pltpu.VMEM((3, 64, 4, 128), F),
            pltpu.VMEM((2, 64, 128), jnp.int32),
            pltpu.VMEM((32, 128), BF),
            pltpu.VMEM((128, 128), BF),
            pltpu.VMEM((4, 128), BF),
            pltpu.VMEM((1, 128), F),
            pltpu.VMEM((1, 128), F),
            pltpu.VMEM((1, 4), F),
            pltpu.SemaphoreType.DMA((8,)),
            pltpu.SemaphoreType.DMA((7,)),
            pltpu.SemaphoreType.DMA,
            pltpu.SemaphoreType.DMA,
            pltpu.SemaphoreType.DMA((4,)),
        ],
        compiler_params=pltpu.CompilerParams(
            collective_id=0, has_side_effects=True, vmem_limit_bytes=40 * 2**20
        ),
    )(
        *(
            pltpu.with_memory_space_constraint(operand, pltpu.HBM)
            for operand in (features, ray_spans.reshape(2, 64, 128))
        ),
        view_order,
        *(
            pltpu.with_memory_space_constraint(operand, pltpu.HBM)
            for operand in (
                w_first.T, w_second, w_last, b_first.reshape(1, 128), b_second.reshape(1, 128), b_last.reshape(1, 4)
            )
        ),
    )


def solution(mesh):
    return jax.shard_map(
        per_device,
        mesh=mesh,
        in_specs=(P(None, "depth", "tile"), P(None, "depth", "tile"), P("tile"), P(), P(), P(), P(), P(), P()),
        out_specs=P(None, ("tile", "depth")),
        check_vma=False,
    )
```

```python
import functools

import jax
import jax.numpy as jnp
from jax import lax
from jax.experimental import pallas as pl
from jax.experimental.pallas import tpu as pltpu
from jax.sharding import PartitionSpec as P

BF = jnp.bfloat16
F = jnp.float32
BRICK = 1024
CH = 32
MESH = pl.DeviceIdType.MESH
AWAY = (4, 3, 5, 2, 6, 1, 7, 0)
RING = tuple(min(a, 8 - a) for a in range(8))
PEERS = sorted(
    ((a, b) for a in range(8) for b in range(8) if a or b), key=lambda p: -(RING[p[0]] + RING[p[1]])
)
FAR = [(a, b) for a, b in PEERS if RING[a] + RING[b] >= 6]


def over(near, far):
    through = 1.0 - near[3]
    return [a + through * b for a, b in zip(near, far)]


def ordered(flip, first, second):
    near = [jnp.where(flip, b, a) for a, b in zip(first, second)]
    far = [jnp.where(flip, a, b) for a, b in zip(first, second)]
    return over(near, far)


def stack_samples(z_ref, spans, zrow, row, flip, b_last, spacing):
    entry = spans[0, pl.ds(row, 8), :]
    leave = spans[1, pl.ds(row, 8), :]
    remain, opacity = [], []
    for s in range(4):
        density = z_ref[pl.ds(zrow + 4 * s, 8, stride=16), :] + b_last[0]
        soft = jnp.maximum(density, 0.0) + jnp.log1p(jnp.exp(-jnp.abs(density)))
        kept = jnp.exp(soft * (-spacing))
        kept = jnp.where((entry <= s) & (leave > s), kept, 1.0)
        remain.append(kept)
        opacity.append(1.0 - kept)
    p01 = remain[0] * remain[1]
    p012 = p01 * remain[2]
    q32 = remain[3] * remain[2]
    q321 = q32 * remain[1]
    through = [
        jnp.where(flip, q321, 1.0),
        jnp.where(flip, q32, remain[0]),
        jnp.where(flip, remain[3], p01),
        jnp.where(flip, 1.0, p012),
    ]
    weight = [t * o for t, o in zip(through, opacity)]
    layers = []
    for ch in range(3):
        total = None
        for s in range(4):
            color = z_ref[pl.ds(zrow + 4 * s + 1 + ch, 8, stride=16), :] + b_last[1 + ch]
            term = weight[s] * (0.5 * jnp.tanh(0.5 * color) + 0.5)
            total = term if total is None else total + term
        layers.append(total)
    layers.append((weight[0] + weight[1]) + (weight[2] + weight[3]))
    return layers


def kernel(*refs, slabs):
    accs = []
    for m in range(2):
        accs += [pltpu.ACC(m)((CH, 256), F)] * 31 + [pltpu.ACC(m)((16, 256), F)] * 2
    pl.run_scoped(lambda *accs: body(*refs, accs=accs, slabs=slabs), *accs)


def body(
    x_hbm, spans_hbm, order, w1_hbm, w2_hbm, w3_hbm, b1_hbm, b2_hbm, bl_hbm, out,
    xbuf, xs, w1p, w2p, w3p, bias, z_ref, h1s, h2s, sent, taken,
    spans, w1t, w2, w3, b1, b2, bl, sem, small_sem, send_sem, hand_sem, recv_sem,
    *, accs, slabs,
):
    acc1 = [accs[m * 33 : m * 33 + 16] for m in range(2)]
    acc2 = [accs[m * 33 + 16 : m * 33 + 31] + accs[m * 33 + 16 : m * 33 + 17] for m in range(2)]
    acc3 = [accs[m * 33 + 31 : m * 33 + 33] for m in range(2)]
    bricks = 8
    me = lax.axis_index("depth")
    low = lax.rem(me, 8)
    high = lax.div(me, 8)
    mirrored = lax.rem(lax.axis_index("tile"), 2) == 1
    spacing = 6.0 / (4 * slabs)

    def place(k):
        step = lax.div(k + 1, 2)
        away = jnp.where(lax.rem(k, 2) == 1, 4 - step, 4 + step)
        return lax.rem(high + jnp.where(mirrored, 8 - away, away), 8)

    def xcopy(k):
        start = pl.multiple_of(place(k) * BRICK, BRICK)
        return pltpu.make_async_copy(x_hbm.at[:, :, pl.ds(start, BRICK)], xbuf.at[k], sem.at[k])

    small = [
        pltpu.make_async_copy(src, dst, small_sem.at[i])
        for i, (src, dst) in enumerate(
            (
                (w1_hbm, w1t), (w2_hbm, w2), (w3_hbm, w3), (b1_hbm, b1), (b2_hbm, b2),
                (bl_hbm, bl), (spans_hbm, spans),
            )
        )
    ]
    for copy in small[:1]:
        copy.start()
    xcopy(0).start()
    for copy in small[1:]:
        copy.start()
    for k in range(1, bricks):
        xcopy(k).start()

    barrier = pltpu.get_barrier_semaphore()

    def greet(dx, dz):
        peer = lax.rem(high + dx, 8) * 8 + lax.rem(low + dz, 8)
        pl.semaphore_signal(barrier, inc=1, device_id={"depth": peer}, device_id_type=MESH)

    @pl.when(low < 6)
    def _():
        for dx, dz in FAR:
            greet(dx, dz)

    for dx, dz in PEERS:
        if (dx, dz) not in FAR:
            greet(dx, dz)

    by_relay = jnp.where(
        (low == 2) | (low == 3), 8, jnp.where((low == 1) | (low == 4), 4, jnp.where((low == 0) | (low == 5), 1, 0))
    )

    for copy in small:
        copy.wait()

    first = jnp.concatenate([w1t[...].astype(F), jnp.zeros((96, 128), F)], axis=0)
    first = jnp.transpose(first).astype(BF)
    first = jnp.concatenate([first, jnp.zeros((128, 128), BF)], axis=1)
    channel = lax.broadcasted_iota(jnp.int32, (256, 128), 0)
    column = lax.broadcasted_iota(jnp.int32, (256, 128), 1)
    for q in range(2):
        spread = jnp.concatenate(
            [(column == channel * 4 + (2 * q + k)).astype(F).astype(BF) for k in range(2)], axis=1
        )
        pltpu.matmul_push_rhs(spread, 0, q)
        for i in range(4):
            rows = first[i * CH : (i + 1) * CH]
            pltpu.matmul_acc_lhs(acc1[q][i], rows, load_staged_rhs=0 if i == 0 else None)
    for q in range(2):
        for i in range(4):
            wide = pltpu.matmul_pop(acc1[q][i]).astype(BF)
            for k in range(2):
                rows = pl.ds(q * 256 + k * 128 + i * CH, CH)
                for j in range(2):
                    w1p[j, rows, j * 128 : (j + 1) * 128] = wide[:, k * 128 : (k + 1) * 128]
                    w1p[j, rows, (1 - j) * 128 : (2 - j) * 128] = jnp.zeros((CH, 128), BF)
    for k in range(2):
        w2p[k * 128 : (k + 1) * 128, k * 128 : (k + 1) * 128] = w2[...]
        w2p[k * 128 : (k + 1) * 128, (1 - k) * 128 : (2 - k) * 128] = jnp.zeros((128, 128), BF)
    last = w3[...].astype(F)
    none = jnp.zeros((4, 128), F)
    for q in range(2):
        left = jnp.concatenate([last if s == 2 * q else none for s in range(4)], axis=0)
        right = jnp.concatenate([last if s == 2 * q + 1 else none for s in range(4)], axis=0)
        w3p[q] = jnp.concatenate([left, right], axis=1).astype(BF)
    bias[0] = jnp.transpose(jnp.broadcast_to(b1[...], (128, 128)))
    bias[1] = jnp.transpose(jnp.broadcast_to(b2[...], (128, 128)))
    flip = jnp.full((8, 128), order[0], jnp.int32) == 1
    b_last = [jnp.broadcast_to(bl[0:1, i : i + 1], (8, 128)) for i in range(4)]

    def prep(k):
        for m in range(2):
            for j in range(2):
                tile = xbuf[k, :, :, m * 512 + j * 256 : m * 512 + (j + 1) * 256]
                xs[lax.rem(k, 2), m, j * 128 : (j + 1) * 128, :] = tile.reshape(128, 256)

    def push(source, stage):
        for m in range(2):
            pltpu.matmul_push_rhs(source(m), stage, m)

    def mm1(j, i, stage):
        for m in range(2):
            rows = w1p[j, i * CH : (i + 1) * CH, :]
            pltpu.matmul_acc_lhs(acc1[m][i], rows, load_staged_rhs=stage if i == 0 else None)

    def mm2(i, stage):
        for m in range(2):
            rows = w2p[(i % 8) * CH : (i % 8 + 1) * CH, :]
            pltpu.matmul_acc_lhs(acc2[m][i], rows, load_staged_rhs=stage if i % 8 == 0 else None)

    def mm3(j, q, stage):
        for m in range(2):
            pltpu.matmul_acc_lhs(acc3[m][j], w3p[q], load_staged_rhs=stage)

    def settle(acc, layer, i, dst):
        r = (i * CH) % 128
        shift = bias[layer, r : r + CH, :]
        shift = jnp.concatenate([shift, shift], axis=1)
        for m in range(2):
            value = (pltpu.matmul_pop(acc[m][i]) + shift).astype(BF)
            dst[m, i * CH : (i + 1) * CH, :] = jnp.maximum(value, jnp.zeros((), BF))

    def pop3(j, par):
        for m in range(2):
            value = pltpu.matmul_pop(acc3[m][j])
            row = par * 128 + 32 * (2 * m + j)
            z_ref[pl.ds(row, 16), :] = value[:, :128]
            z_ref[pl.ds(row + 16, 16), :] = value[:, 128:]

    def slot(k, j, first=False, second=False, last=False, last_brick=False, middle=None, late=None):
        par = lax.rem(k, 2)
        s0, s1 = j % 2, 1 - j % 2
        push(lambda m: h1s[m, 0:256, :], s1)
        for i in range(16):
            if not last:
                mm1(1 - j, i, s0)
            if i >= 1 and not first:
                settle(acc2, 1, i, h2s)
            if i == 8 and not first:
                push(lambda m: h2s[m, 0:256, :], s0)
        if middle:
            middle()
        if not first and not second:
            pop3(j, 1 - par)
        for i in range(8):
            mm2(i, s1)
            if not last:
                settle(acc1, 0, i, h1s)
        push(lambda m: h1s[m, 256:512, :], s1)
        if not first:
            mm3(1 - j, 0, s0)
            push(lambda m: h2s[m, 256:512, :], s0)
        for i in range(8, 16):
            if i == 15:
                settle(acc2, 1, 0, h2s)
            mm2(i, s1)
            if not last:
                settle(acc1, 0, i, h1s)
        if late:
            late()
        if not last_brick:
            push(lambda m: xs[1 - par, m], s1)
        if not first:
            mm3(1 - j, 1, s0)

    def brick(k, first=False, last=False, late=None):
        if not last:
            xcopy(k + 1).wait()
        middle = None if last else lambda: prep(k + 1)
        slot(k, 0, first=first, last_brick=last, middle=middle)
        slot(k, 1, second=first, last=last, last_brick=last, late=late)

    def send(k, j):
        chunk = lax.rem(low + jnp.where(mirrored, 8 - AWAY[j], AWAY[j]), 8)
        owner = place(k) * 8 + chunk
        way, target = 0, owner
        if RING[AWAY[j]] >= 2:
            far = (chunk >= 6) & (4 - lax.div(k + 1, 2) >= 6 - RING[AWAY[j]])
            way = jnp.where(far, 8 - chunk, 0)
            target = jnp.where(far, place(k) * 8, owner)
        return pltpu.make_async_remote_copy(
            src_ref=sent.at[k * 8 + chunk],
            dst_ref=taken.at[way, me],
            send_sem=send_sem,
            recv_sem=recv_sem.at[way],
            device_id={"depth": target},
            device_id_type=MESH,
        )

    def arrived(way, count):
        pltpu.make_async_remote_copy(
            src_ref=sent.at[pl.ds(0, count)],
            dst_ref=taken.at[0, pl.ds(0, count)],
            send_sem=send_sem,
            recv_sem=recv_sem.at[way],
            device_id={"depth": lax.rem(me + 1, slabs)},
            device_id_type=MESH,
        ).wait_recv()

    def hand_on(way):
        arrived(way, len(FAR))
        for dx, dz in FAR:
            source = lax.rem(high + 8 - dx, 8) * 8 + (16 - way - dz) % 8
            pltpu.make_async_remote_copy(
                src_ref=taken.at[way, source],
                dst_ref=taken.at[0, source],
                send_sem=hand_sem,
                recv_sem=recv_sem.at[3],
                device_id={"depth": high * 8 + 8 - way},
                device_id_type=MESH,
            ).start()

    def finish(k):
        row = pl.multiple_of(place(k) * 8, 8)
        layers = stack_samples(z_ref, spans, lax.rem(k, 2) * 128, row, flip, b_last, spacing)
        for ch in range(4):
            sent[pl.ds(k * 8, 8), ch, :] = layers[ch]

    def send_brick(k):
        for j in range(8):
            send(k, j).start()

    xcopy(0).wait()
    prep(0)
    push(lambda m: xs[0, m], 1)
    for i in range(16):
        mm1(0, i, 1)
    push(lambda m: xs[0, m], 0)
    for i in range(16):
        settle(acc1, 0, i, h1s)
    brick(0, first=True)

    def step(k, _):
        brick(k, late=lambda: finish(k - 1))

        @pl.when(k == 2)
        def _():
            pl.semaphore_wait(barrier, slabs - 1 - by_relay)
            send_brick(0)

        @pl.when(k >= 2)
        def _():
            send_brick(k - 1)

        return 0

    lax.fori_loop(1, bricks - 1, step, 0)
    brick(bricks - 1, last=True, late=lambda: finish(bricks - 2))
    send_brick(bricks - 2)
    for i in range(1, 16):
        settle(acc2, 1, i, h2s)
    push(lambda m: h2s[m, 0:256, :], 0)
    push(lambda m: h2s[m, 256:512, :], 1)
    pop3(0, (bricks - 1) % 2)
    mm3(1, 0, 0)
    mm3(1, 1, 1)
    pop3(1, (bricks - 1) % 2)
    finish(bricks - 1)
    for j in range(7):
        send(bricks - 1, j).start()
    taken[0, me] = sent[(bricks - 1) * 8 + low]

    @pl.when(low == 0)
    def _():
        hand_on(2)
        hand_on(1)

    @pl.when(low < 6)
    def _():
        arrived(0, slabs - 1)

    @pl.when(low >= 6)
    def _():
        arrived(0, slabs - 1 - len(FAR))
        arrived(3, len(FAR))

    groups = [[taken[0, pl.ds(k, 8, stride=8), ch, :] for ch in range(4)] for k in range(8)]
    while len(groups) > 1:
        groups = [ordered(flip, a, b) for a, b in zip(groups[::2], groups[1::2])]
    total = groups[0]
    for shift in (7, 6, 4):
        total = ordered(flip, total, [pltpu.roll(c, shift, 0) for c in total])
    out[...] = jnp.concatenate([c[0:1] for c in total], axis=0)
    pltpu.make_async_remote_copy(
        src_ref=sent.at[pl.ds(0, slabs - 1)],
        dst_ref=taken.at[0, pl.ds(0, slabs - 1)],
        send_sem=send_sem,
        recv_sem=recv_sem.at[0],
        device_id={"depth": lax.rem(me + 1, slabs)},
        device_id_type=MESH,
    ).wait_send()

    @pl.when(low == 0)
    def _():
        pltpu.make_async_remote_copy(
            src_ref=sent.at[pl.ds(0, 2 * len(FAR))],
            dst_ref=taken.at[0, pl.ds(0, 2 * len(FAR))],
            send_sem=hand_sem,
            recv_sem=recv_sem.at[3],
            device_id={"depth": lax.rem(me + 1, slabs)},
            device_id_type=MESH,
        ).wait_send()


def per_device(features, ray_spans, view_order, w_first, b_first, w_second, b_second, w_last, b_last):
    slabs = lax.axis_size("depth")
    hbm = pl.BlockSpec(memory_space=pltpu.HBM)
    return pl.pallas_call(
        functools.partial(kernel, slabs=slabs),
        out_shape=jax.ShapeDtypeStruct((4, 128), F),
        in_specs=[hbm, hbm, pl.BlockSpec(memory_space=pltpu.SMEM)] + [hbm] * 6,
        out_specs=pl.BlockSpec(memory_space=pltpu.VMEM),
        scratch_shapes=[
            pltpu.VMEM((8, 32, 4, BRICK), BF),
            pltpu.VMEM((2, 2, 256, 256), BF),
            pltpu.VMEM((2, 512, 256), BF),
            pltpu.VMEM((256, 256), BF),
            pltpu.VMEM((2, 16, 256), BF),
            pltpu.VMEM((2, 128, 128), F),
            pltpu.VMEM((2 * 8 * 16, 128), F),
            pltpu.VMEM((2, 512, 256), BF),
            pltpu.VMEM((2, 512, 256), BF),
            pltpu.VMEM((64, 4, 128), F),
            pltpu.VMEM((3, 64, 4, 128), F),
            pltpu.VMEM((2, 64, 128), jnp.int32),
            pltpu.VMEM((32, 128), BF),
            pltpu.VMEM((128, 128), BF),
            pltpu.VMEM((4, 128), BF),
            pltpu.VMEM((1, 128), F),
            pltpu.VMEM((1, 128), F),
            pltpu.VMEM((1, 4), F),
            pltpu.SemaphoreType.DMA((8,)),
            pltpu.SemaphoreType.DMA((7,)),
            pltpu.SemaphoreType.DMA,
            pltpu.SemaphoreType.DMA,
            pltpu.SemaphoreType.DMA((4,)),
        ],
        compiler_params=pltpu.CompilerParams(
            collective_id=0, has_side_effects=True, vmem_limit_bytes=40 * 2**20
        ),
    )(
        *(
            pltpu.with_memory_space_constraint(operand, pltpu.HBM)
            for operand in (features, ray_spans.reshape(2, 64, 128))
        ),
        view_order,
        *(
            pltpu.with_memory_space_constraint(operand, pltpu.HBM)
            for operand in (
                w_first.T, w_second, w_last, b_first.reshape(1, 128), b_second.reshape(1, 128), b_last.reshape(1, 4)
            )
        ),
    )


def solution(mesh):
    return jax.shard_map(
        per_device,
        mesh=mesh,
        in_specs=(P(None, "depth", "tile"), P(None, "depth", "tile"), P("tile"), P(), P(), P(), P(), P(), P()),
        out_specs=P(None, ("tile", "depth")),
        check_vma=False,
    )
```

```python
import functools

import jax
import jax.numpy as jnp
from jax import lax
from jax.experimental import pallas as pl
from jax.experimental.pallas import tpu as pltpu
from jax.sharding import PartitionSpec as P

BF = jnp.bfloat16
F = jnp.float32
BRICK = 1024
CH = 32
MESH = pl.DeviceIdType.MESH
AWAY = (4, 3, 5, 2, 6, 1, 7, 0)
RING = tuple(min(a, 8 - a) for a in range(8))
PEERS = sorted(
    ((a, b) for a in range(8) for b in range(8) if a or b), key=lambda p: -(RING[p[0]] + RING[p[1]])
)
FAR = [(a, b) for a, b in PEERS if RING[a] + RING[b] >= 6]


def over(near, far):
    through = 1.0 - near[3]
    return [a + through * b for a, b in zip(near, far)]


def ordered(flip, first, second):
    near = [jnp.where(flip, b, a) for a, b in zip(first, second)]
    far = [jnp.where(flip, a, b) for a, b in zip(first, second)]
    return over(near, far)


def stack_samples(z_ref, spans, zrow, row, flip, b_last, spacing):
    entry = spans[0, pl.ds(row, 8), :]
    leave = spans[1, pl.ds(row, 8), :]
    remain, opacity = [], []
    for s in range(4):
        density = z_ref[pl.ds(zrow + 4 * s, 8, stride=16), :] + b_last[0]
        soft = jnp.maximum(density, 0.0) + jnp.log1p(jnp.exp(-jnp.abs(density)))
        kept = jnp.exp(soft * (-spacing))
        kept = jnp.where((entry <= s) & (leave > s), kept, 1.0)
        remain.append(kept)
        opacity.append(1.0 - kept)
    p01 = remain[0] * remain[1]
    p012 = p01 * remain[2]
    q32 = remain[3] * remain[2]
    q321 = q32 * remain[1]
    through = [
        jnp.where(flip, q321, 1.0),
        jnp.where(flip, q32, remain[0]),
        jnp.where(flip, remain[3], p01),
        jnp.where(flip, 1.0, p012),
    ]
    weight = [t * o for t, o in zip(through, opacity)]
    layers = []
    for ch in range(3):
        total = None
        for s in range(4):
            color = z_ref[pl.ds(zrow + 4 * s + 1 + ch, 8, stride=16), :] + b_last[1 + ch]
            term = weight[s] * (0.5 * jnp.tanh(0.5 * color) + 0.5)
            total = term if total is None else total + term
        layers.append(total)
    layers.append((weight[0] + weight[1]) + (weight[2] + weight[3]))
    return layers


def kernel(*refs, slabs):
    accs = []
    for m in range(2):
        accs += [pltpu.ACC(m)((CH, 256), F)] * 31 + [pltpu.ACC(m)((16, 256), F)] * 2
    pl.run_scoped(lambda *accs: body(*refs, accs=accs, slabs=slabs), *accs)


def body(
    x_hbm, spans_hbm, order, w1_hbm, w2_hbm, w3_hbm, b1_hbm, b2_hbm, bl_hbm, out,
    xbuf, xs, w1p, w2p, w3p, bias, z_ref, h1s, h2s, sent, taken,
    spans, w1t, w2, w3, b1, b2, bl, sem, small_sem, send_sem, hand_sem, recv_sem,
    *, accs, slabs,
):
    acc1 = [accs[m * 33 : m * 33 + 16] for m in range(2)]
    acc2 = [accs[m * 33 + 16 : m * 33 + 31] + accs[m * 33 + 16 : m * 33 + 17] for m in range(2)]
    acc3 = [accs[m * 33 + 31 : m * 33 + 33] for m in range(2)]
    bricks = 8
    me = lax.axis_index("depth")
    low = lax.rem(me, 8)
    high = lax.div(me, 8)
    mirrored = lax.rem(lax.axis_index("tile"), 2) == 1
    spacing = 6.0 / (4 * slabs)

    def place(k):
        step = lax.div(k + 1, 2)
        away = jnp.where(lax.rem(k, 2) == 1, 4 - step, 4 + step)
        return lax.rem(high + jnp.where(mirrored, 8 - away, away), 8)

    def xcopy(k):
        start = pl.multiple_of(place(k) * BRICK, BRICK)
        return pltpu.make_async_copy(x_hbm.at[:, :, pl.ds(start, BRICK)], xbuf.at[k], sem.at[k])

    small = [
        pltpu.make_async_copy(src, dst, small_sem.at[i])
        for i, (src, dst) in enumerate(
            (
                (w1_hbm, w1t), (w2_hbm, w2), (w3_hbm, w3), (b1_hbm, b1), (b2_hbm, b2),
                (bl_hbm, bl), (spans_hbm, spans),
            )
        )
    ]
    for copy in small[:1]:
        copy.start()
    xcopy(0).start()
    for copy in small[1:]:
        copy.start()
    for k in range(1, bricks):
        xcopy(k).start()

    barrier = pltpu.get_barrier_semaphore()

    def greet(dx, dz):
        peer = lax.rem(high + dx, 8) * 8 + lax.rem(low + dz, 8)
        pl.semaphore_signal(barrier, inc=1, device_id={"depth": peer}, device_id_type=MESH)

    @pl.when(low < 6)
    def _():
        for dx, dz in FAR:
            greet(dx, dz)

    for dx, dz in PEERS:
        if (dx, dz) not in FAR:
            greet(dx, dz)

    by_relay = jnp.where(
        (low == 2) | (low == 3), 8, jnp.where((low == 1) | (low == 4), 4, jnp.where((low == 0) | (low == 5), 1, 0))
    )

    for copy in small:
        copy.wait()

    first = jnp.concatenate([w1t[...].astype(F), jnp.zeros((96, 128), F)], axis=0)
    first = jnp.transpose(first).astype(BF)
    first = jnp.concatenate([first, jnp.zeros((128, 128), BF)], axis=1)
    channel = lax.broadcasted_iota(jnp.int32, (256, 128), 0)
    column = lax.broadcasted_iota(jnp.int32, (256, 128), 1)
    for q in range(2):
        spread = jnp.concatenate(
            [(column == channel * 4 + (2 * q + k)).astype(F).astype(BF) for k in range(2)], axis=1
        )
        pltpu.matmul_push_rhs(spread, 0, q)
        for i in range(4):
            rows = first[i * CH : (i + 1) * CH]
            pltpu.matmul_acc_lhs(acc1[q][i], rows, load_staged_rhs=0 if i == 0 else None)
    for q in range(2):
        for i in range(4):
            wide = pltpu.matmul_pop(acc1[q][i]).astype(BF)
            for k in range(2):
                rows = pl.ds(q * 256 + k * 128 + i * CH, CH)
                for j in range(2):
                    w1p[j, rows, j * 128 : (j + 1) * 128] = wide[:, k * 128 : (k + 1) * 128]
                    w1p[j, rows, (1 - j) * 128 : (2 - j) * 128] = jnp.zeros((CH, 128), BF)
    for k in range(2):
        w2p[k * 128 : (k + 1) * 128, k * 128 : (k + 1) * 128] = w2[...]
        w2p[k * 128 : (k + 1) * 128, (1 - k) * 128 : (2 - k) * 128] = jnp.zeros((128, 128), BF)
    last = w3[...].astype(F)
    none = jnp.zeros((4, 128), F)
    for q in range(2):
        left = jnp.concatenate([last if s == 2 * q else none for s in range(4)], axis=0)
        right = jnp.concatenate([last if s == 2 * q + 1 else none for s in range(4)], axis=0)
        w3p[q] = jnp.concatenate([left, right], axis=1).astype(BF)
    bias[0] = jnp.transpose(jnp.broadcast_to(b1[...], (128, 128)))
    bias[1] = jnp.transpose(jnp.broadcast_to(b2[...], (128, 128)))
    flip = jnp.full((8, 128), order[0], jnp.int32) == 1
    b_last = [jnp.broadcast_to(bl[0:1, i : i + 1], (8, 128)) for i in range(4)]

    def prep(k):
        for m in range(2):
            for j in range(2):
                tile = xbuf[k, :, :, m * 512 + j * 256 : m * 512 + (j + 1) * 256]
                xs[lax.rem(k, 2), m, j * 128 : (j + 1) * 128, :] = tile.reshape(128, 256)

    def push(source, stage):
        for m in range(2):
            pltpu.matmul_push_rhs(source(m), stage, m)

    def mm1(j, i, stage):
        for m in range(2):
            rows = w1p[j, i * CH : (i + 1) * CH, :]
            pltpu.matmul_acc_lhs(acc1[m][i], rows, load_staged_rhs=stage if i == 0 else None)

    def mm2(i, stage):
        for m in range(2):
            rows = w2p[(i % 8) * CH : (i % 8 + 1) * CH, :]
            pltpu.matmul_acc_lhs(acc2[m][i], rows, load_staged_rhs=stage if i % 8 == 0 else None)

    def mm3(j, q, stage):
        for m in range(2):
            pltpu.matmul_acc_lhs(acc3[m][j], w3p[q], load_staged_rhs=stage)

    def settle(acc, layer, i, dst):
        r = (i * CH) % 128
        shift = bias[layer, r : r + CH, :]
        shift = jnp.concatenate([shift, shift], axis=1)
        for m in range(2):
            value = (pltpu.matmul_pop(acc[m][i]) + shift).astype(BF)
            dst[m, i * CH : (i + 1) * CH, :] = jnp.maximum(value, jnp.zeros((), BF))

    def pop3(j, par):
        for m in range(2):
            value = pltpu.matmul_pop(acc3[m][j])
            row = par * 128 + 32 * (2 * m + j)
            z_ref[pl.ds(row, 16), :] = value[:, :128]
            z_ref[pl.ds(row + 16, 16), :] = value[:, 128:]

    def slot(k, j, first=False, second=False, last=False, last_brick=False, middle=None, late=None):
        par = lax.rem(k, 2)
        s0, s1 = j % 2, 1 - j % 2
        push(lambda m: h1s[m, 0:256, :], s1)
        for i in range(16):
            if not last:
                mm1(1 - j, i, s0)
            if i >= 1 and not first:
                settle(acc2, 1, i, h2s)
            if i == 8 and not first:
                push(lambda m: h2s[m, 0:256, :], s0)
        if middle:
            middle()
        if not first and not second:
            pop3(j, 1 - par)
        for i in range(8):
            mm2(i, s1)
            if not last:
                settle(acc1, 0, i, h1s)
        push(lambda m: h1s[m, 256:512, :], s1)
        if not first:
            mm3(1 - j, 0, s0)
            push(lambda m: h2s[m, 256:512, :], s0)
        for i in range(8, 16):
            if i == 15:
                settle(acc2, 1, 0, h2s)
            mm2(i, s1)
            if not last:
                settle(acc1, 0, i, h1s)
        if late:
            late()
        if not last_brick:
            push(lambda m: xs[1 - par, m], s1)
        if not first:
            mm3(1 - j, 1, s0)

    def brick(k, first=False, last=False, late=None):
        if not last:
            xcopy(k + 1).wait()
        middle = None if last else lambda: prep(k + 1)
        slot(k, 0, first=first, last_brick=last, middle=middle)
        slot(k, 1, second=first, last=last, last_brick=last, late=late)

    def send(k, j):
        chunk = lax.rem(low + jnp.where(mirrored, 8 - AWAY[j], AWAY[j]), 8)
        owner = place(k) * 8 + chunk
        way, target = 0, owner
        if RING[AWAY[j]] >= 2:
            far = (chunk >= 6) & (4 - lax.div(k + 1, 2) >= 6 - RING[AWAY[j]])
            way = jnp.where(far, 8 - chunk, 0)
            target = jnp.where(far, place(k) * 8, owner)
        return pltpu.make_async_remote_copy(
            src_ref=sent.at[k * 8 + chunk],
            dst_ref=taken.at[way, me],
            send_sem=send_sem,
            recv_sem=recv_sem.at[way],
            device_id={"depth": target},
            device_id_type=MESH,
        )

    def arrived(way, count):
        pltpu.make_async_remote_copy(
            src_ref=sent.at[pl.ds(0, count)],
            dst_ref=taken.at[0, pl.ds(0, count)],
            send_sem=send_sem,
            recv_sem=recv_sem.at[way],
            device_id={"depth": lax.rem(me + 1, slabs)},
            device_id_type=MESH,
        ).wait_recv()

    def hand_on(way):
        arrived(way, len(FAR))
        for dx, dz in FAR:
            source = lax.rem(high + 8 - dx, 8) * 8 + (16 - way - dz) % 8
            pltpu.make_async_remote_copy(
                src_ref=taken.at[way, source],
                dst_ref=taken.at[0, source],
                send_sem=hand_sem,
                recv_sem=recv_sem.at[3],
                device_id={"depth": high * 8 + 8 - way},
                device_id_type=MESH,
            ).start()

    def finish(k):
        row = pl.multiple_of(place(k) * 8, 8)
        layers = stack_samples(z_ref, spans, lax.rem(k, 2) * 128, row, flip, b_last, spacing)
        for ch in range(4):
            sent[pl.ds(k * 8, 8), ch, :] = layers[ch]

    def send_brick(k):
        for j in range(8):
            send(k, j).start()

    xcopy(0).wait()
    prep(0)
    push(lambda m: xs[0, m], 1)
    for i in range(16):
        mm1(0, i, 1)
    push(lambda m: xs[0, m], 0)
    for i in range(16):
        settle(acc1, 0, i, h1s)
    brick(0, first=True)

    def step(k, _):
        brick(k, late=lambda: finish(k - 1))

        @pl.when(k == 4)
        def _():
            pl.semaphore_wait(barrier, slabs - 1 - by_relay)
            send_brick(0)
            send_brick(1)
            send_brick(2)

        @pl.when(k >= 4)
        def _():
            send_brick(k - 1)

        return 0

    lax.fori_loop(1, bricks - 1, step, 0)
    brick(bricks - 1, last=True, late=lambda: finish(bricks - 2))
    send_brick(bricks - 2)
    for i in range(1, 16):
        settle(acc2, 1, i, h2s)
    push(lambda m: h2s[m, 0:256, :], 0)
    push(lambda m: h2s[m, 256:512, :], 1)
    pop3(0, (bricks - 1) % 2)
    mm3(1, 0, 0)
    mm3(1, 1, 1)
    pop3(1, (bricks - 1) % 2)
    finish(bricks - 1)
    for j in range(7):
        send(bricks - 1, j).start()
    taken[0, me] = sent[(bricks - 1) * 8 + low]

    @pl.when(low == 0)
    def _():
        hand_on(2)
        hand_on(1)

    @pl.when(low < 6)
    def _():
        arrived(0, slabs - 1)

    @pl.when(low >= 6)
    def _():
        arrived(0, slabs - 1 - len(FAR))
        arrived(3, len(FAR))

    groups = [[taken[0, pl.ds(k, 8, stride=8), ch, :] for ch in range(4)] for k in range(8)]
    while len(groups) > 1:
        groups = [ordered(flip, a, b) for a, b in zip(groups[::2], groups[1::2])]
    total = groups[0]
    for shift in (7, 6, 4):
        total = ordered(flip, total, [pltpu.roll(c, shift, 0) for c in total])
    out[...] = jnp.concatenate([c[0:1] for c in total], axis=0)
    pltpu.make_async_remote_copy(
        src_ref=sent.at[pl.ds(0, slabs - 1)],
        dst_ref=taken.at[0, pl.ds(0, slabs - 1)],
        send_sem=send_sem,
        recv_sem=recv_sem.at[0],
        device_id={"depth": lax.rem(me + 1, slabs)},
        device_id_type=MESH,
    ).wait_send()

    @pl.when(low == 0)
    def _():
        pltpu.make_async_remote_copy(
            src_ref=sent.at[pl.ds(0, 2 * len(FAR))],
            dst_ref=taken.at[0, pl.ds(0, 2 * len(FAR))],
            send_sem=hand_sem,
            recv_sem=recv_sem.at[3],
            device_id={"depth": lax.rem(me + 1, slabs)},
            device_id_type=MESH,
        ).wait_send()


def per_device(features, ray_spans, view_order, w_first, b_first, w_second, b_second, w_last, b_last):
    slabs = lax.axis_size("depth")
    hbm = pl.BlockSpec(memory_space=pltpu.HBM)
    return pl.pallas_call(
        functools.partial(kernel, slabs=slabs),
        out_shape=jax.ShapeDtypeStruct((4, 128), F),
        in_specs=[hbm, hbm, pl.BlockSpec(memory_space=pltpu.SMEM)] + [hbm] * 6,
        out_specs=pl.BlockSpec(memory_space=pltpu.VMEM),
        scratch_shapes=[
            pltpu.VMEM((8, 32, 4, BRICK), BF),
            pltpu.VMEM((2, 2, 256, 256), BF),
            pltpu.VMEM((2, 512, 256), BF),
            pltpu.VMEM((256, 256), BF),
            pltpu.VMEM((2, 16, 256), BF),
            pltpu.VMEM((2, 128, 128), F),
            pltpu.VMEM((2 * 8 * 16, 128), F),
            pltpu.VMEM((2, 512, 256), BF),
            pltpu.VMEM((2, 512, 256), BF),
            pltpu.VMEM((64, 4, 128), F),
            pltpu.VMEM((3, 64, 4, 128), F),
            pltpu.VMEM((2, 64, 128), jnp.int32),
            pltpu.VMEM((32, 128), BF),
            pltpu.VMEM((128, 128), BF),
            pltpu.VMEM((4, 128), BF),
            pltpu.VMEM((1, 128), F),
            pltpu.VMEM((1, 128), F),
            pltpu.VMEM((1, 4), F),
            pltpu.SemaphoreType.DMA((8,)),
            pltpu.SemaphoreType.DMA((7,)),
            pltpu.SemaphoreType.DMA,
            pltpu.SemaphoreType.DMA,
            pltpu.SemaphoreType.DMA((4,)),
        ],
        compiler_params=pltpu.CompilerParams(
            collective_id=0, has_side_effects=True, vmem_limit_bytes=40 * 2**20
        ),
    )(
        *(
            pltpu.with_memory_space_constraint(operand, pltpu.HBM)
            for operand in (features, ray_spans.reshape(2, 64, 128))
        ),
        view_order,
        *(
            pltpu.with_memory_space_constraint(operand, pltpu.HBM)
            for operand in (
                w_first.T, w_second, w_last, b_first.reshape(1, 128), b_second.reshape(1, 128), b_last.reshape(1, 4)
            )
        ),
    )


def solution(mesh):
    return jax.shard_map(
        per_device,
        mesh=mesh,
        in_specs=(P(None, "depth", "tile"), P(None, "depth", "tile"), P("tile"), P(), P(), P(), P(), P(), P()),
        out_specs=P(None, ("tile", "depth")),
        check_vma=False,
    )
```
